32 devices in a mesh: req: 4 (over x, core), kv: 8 (over z, y).
Axes of the slice: x: 2, y: 2, z: 4, core: 2. Of those that a mesh axis runs over, the one named last changes fastest.
Arguments:
- x_steps: bfloat16 [4, 256, 1536], P(None, ('req', 'kv')), may hold values from -6 to 6
- lengths: int32 [32], replicated, may hold values from 16 to 8192
- perm: int32 [32], replicated, may hold values from 0 to 31, as said below
- parents: int32 [4, 256], replicated, may hold values from 0 to 7
- table: int32 [256, 9], P(('req', 'kv')), may hold values from 0 to 2303, as said below
- pool: bfloat16 [2304, 128, 256], P(('req', 'kv')), may hold values from -900 to 900
- norm_attn: float32 [1536], replicated, may hold values from 0.1 to 1.9
- w_query: bfloat16 [1536, 1536], replicated, may hold values from -0.15625 to 0.15625
- w_keyval: bfloat16 [1536, 256], replicated, may hold values from -0.15625 to 0.15625
- w_out: bfloat16 [1536, 1536], replicated, may hold values from -0.15625 to 0.15625
- norm_mlp: float32 [1536], replicated, may hold values from 0.1 to 1.9
- w_gate: bfloat16 [1536, 4608], P(None, 'kv'), may hold values from -0.15625 to 0.15625
- w_up: bfloat16 [1536, 4608], P(None, 'kv'), may hold values from -0.15625 to 0.15625
- w_down: bfloat16 [4608, 1536], P('kv'), may hold values from -0.09375 to 0.09375
Outputs:
- outputs: bfloat16 [4, 256, 1536], P(None, ('req', 'kv'))
The draws below stay inside these ranges and needn't reach their ends.
Inputs may be any that keep to these rules, and one draw needn't show every extreme that they name: perm is a permutation with perm[s] % 8 == s % 8; among the 8 slots s with one s // 8 and one s % 8 // 8, every req index occurs as perm[s] // 8 exactly once. The entries of row b lie in [(b // 8) * 72, (b // 8 + 1) * 72); no page appears twice in the table.
All inputs are finite; a program needn't handle non-finite values.
Results may differ from the reference program's by a relative error of at most 0.02.
Values may be sent and summed in bfloat16 or wider, within the bound.
A program may use at most 192 MiB of HBM per device.

```python
import jax
import jax.numpy as jnp
from jax import lax

D = 1536
HEADS = 12
HEAD_DIM = 128
FF = 4608
WINDOW = 1024
PAGE = 128
BEAMS = 8
STEPS = 4
LMAX = 8192
RQH = 8
WPAGES = 9
RQ = 8
REQS = 32
ROWS = 256
PAGES_DEV = 72
PAGES = 2304
N_REQ = 4
N_KV = 8


def draw_lengths(key, part):
    choose_key, short_key, long_key, marked_key = jax.random.split(key, 4)
    chosen = jax.random.randint(choose_key, (REQS,), 0, 2)
    short_len = jax.random.randint(short_key, (REQS,), 16, WINDOW)
    long_len = jax.random.randint(long_key, (REQS,), WINDOW, LMAX + 1)
    values = jnp.where(chosen == 1, long_len, short_len)
    marked = jax.random.randint(marked_key, (), 0, REQS)
    values = values.at[marked].set(LMAX)
    values = values.at[(marked + 1) % REQS].set(16)
    return values.astype(jnp.int32)


def draw_perm(key, part):
    halves = N_KV // BEAMS
    per_group = RQH * halves
    half_keys = jax.random.split(key, halves)
    shifts = jax.vmap(lambda one_key: jax.random.permutation(one_key, jnp.arange(RQH, dtype=jnp.int32) % N_REQ))(half_keys)
    shifts = shifts.reshape(per_group)
    groups = jnp.arange(N_REQ, dtype=jnp.int32)
    offsets = jnp.arange(per_group, dtype=jnp.int32)
    values = (groups[:, None] + shifts[None, :]) % N_REQ * per_group + offsets[None, :]
    return values.reshape(N_REQ * per_group).astype(jnp.int32)


def draw_table(key, part):
    device_count = N_REQ * N_KV
    device_keys = jax.random.split(key, device_count)
    shuffled = jax.vmap(lambda one_key: jax.random.permutation(one_key, PAGES_DEV))(device_keys)
    owner = jnp.arange(device_count, dtype=jnp.int32)[:, None] * PAGES_DEV
    return (owner + shuffled.astype(jnp.int32)).reshape(device_count * RQH, WPAGES).astype(jnp.int32)


def draw_pool(key, part):
    base_key = jax.random.fold_in(key, 0)
    values = jnp.clip(jax.random.normal(base_key, (PAGES, PAGE // 2, 2, 2 * HEAD_DIM), jnp.float32), -6.0, 6.0)
    return values.reshape(PAGES, PAGE, 2 * HEAD_DIM).astype(jnp.bfloat16)


def place_ends(drawn, key, low, largest):
    spot = [jax.random.randint(jax.random.fold_in(key, axis), (), 0, length) for axis, length in enumerate(drawn.shape)]
    widest = drawn.shape.index(max(drawn.shape))
    next_to = spot[:widest] + [(spot[widest] + 1) % drawn.shape[widest]] + spot[widest + 1:]
    return drawn.at[tuple(spot)].set(low).at[tuple(next_to)].set(largest)


def level_of(stream_key, shape, shards, least, largest):
    factor_of = 1.0
    for position, shards_of in shards:
        heights = jax.random.uniform(jax.random.fold_in(jax.random.fold_in(stream_key, 6), position), (shards_of,), jnp.float32, least / len(shards), largest / len(shards))
        factor_of = factor_of * jnp.repeat(jnp.exp(heights), shape[position] // shards_of).reshape((-1,) + (1,) * (len(shape) - 1 - position))
    return factor_of


def noise(own_key, shape, deviation, reach, pieces=(), kind=jnp.bfloat16):
    values = jax.random.normal(own_key, shape, jnp.float32) * deviation
    if len(pieces) > 0:
        values = level_of(own_key, shape, pieces, -0.22, 0.18) * values
    return jnp.clip(values, min=-reach, max=reach).astype(kind)


def setup_inputs(seed: int = 0) -> dict:
    streams_of = jax.random.split(jax.random.key(seed), 15)
    x_steps = noise(streams_of[0], (STEPS, ROWS, D), 1.0, 6.0, ((1, 32),))
    lengths = draw_lengths(jax.random.fold_in(streams_of[14], 71), 0)
    perm = draw_perm(jax.random.fold_in(streams_of[14], 71), 0)
    parents = place_ends(jax.random.randint(streams_of[3], (STEPS, ROWS), 0, BEAMS), jax.random.fold_in(streams_of[3], 1), 0, BEAMS - 1).astype(jnp.int32)
    table = draw_table(jax.random.fold_in(streams_of[14], 71), 0)
    pool = draw_pool(jax.random.fold_in(streams_of[14], 71), 0)
    norm_attn = jnp.clip(1.0 + 0.18 * jax.random.normal(streams_of[6], (D,), jnp.float32), 0.1, 1.9)
    w_query = noise(streams_of[7], (D, HEADS * HEAD_DIM), D ** -0.5, 0.15625)
    w_keyval = noise(streams_of[8], (D, 2 * HEAD_DIM), D ** -0.5, 0.15625)
    w_out = noise(streams_of[9], (HEADS * HEAD_DIM, D), (HEADS * HEAD_DIM) ** -0.5, 0.15625)
    norm_mlp = jnp.clip(1.0 + 0.18 * jax.random.normal(streams_of[10], (D,), jnp.float32), 0.1, 1.9)
    w_gate = noise(streams_of[11], (D, FF), D ** -0.5, 0.15625, ((1, 8),))
    w_up = noise(streams_of[12], (D, FF), D ** -0.5, 0.15625, ((1, 8),))
    w_down = noise(streams_of[13], (FF, D), FF ** -0.5, 0.09375, ((0, 8),))
    return {"x_steps": x_steps, "lengths": lengths, "perm": perm, "parents": parents, "table": table, "pool": pool, "norm_attn": norm_attn, "w_query": w_query, "w_keyval": w_keyval, "w_out": w_out, "norm_mlp": norm_mlp, "w_gate": w_gate, "w_up": w_up, "w_down": w_down}


EPSILON = 1e-06
NEGATIVE = -1e+30

def member_of(beam_index, half_index, halves):
    return beam_index % 2 + 2 * half_index + 2 * halves * (beam_index // 2)

def rms_round(values, gain):
    wide = values.astype(jnp.float32)
    mean_square = lax.optimization_barrier(jnp.mean(wide * wide, axis=-1, keepdims=True))
    return (wide * lax.rsqrt(mean_square + EPSILON) * gain).astype(jnp.bfloat16)

def page_partial(queries, pages, key_pos, length, step_index):
    head_dim = queries.shape[-1]
    keys = pages[:, :, :head_dim].astype(jnp.float32)
    values = pages[:, :, head_dim:].astype(jnp.float32)
    scores = jnp.einsum('rhd,rkd->rhk', queries.astype(jnp.float32), keys) * head_dim ** (-0.5)
    allowed = (key_pos < length[:, None]) & (key_pos > length[:, None] + step_index - WINDOW)
    scores = jnp.where(allowed[:, None, :], scores, NEGATIVE)
    highest = lax.optimization_barrier(jnp.max(scores, axis=-1))
    weights = jnp.exp(scores - highest[..., None]).astype(jnp.bfloat16)
    totals = lax.optimization_barrier(jnp.sum(weights.astype(jnp.float32), axis=-1))
    weighted = jnp.einsum('rhk,rkd->rhd', weights.astype(jnp.float32), values)
    return (highest, totals, weighted)

def fresh_partial(queries, entries, count):
    head_dim = queries.shape[-1]
    keys = entries[:, :count, :head_dim].astype(jnp.float32)
    values = entries[:, :count, head_dim:].astype(jnp.float32)
    scores = jnp.einsum('rhd,rkd->rhk', queries.astype(jnp.float32), keys) * head_dim ** (-0.5)
    highest = lax.optimization_barrier(jnp.max(scores, axis=-1))
    weights = jnp.exp(scores - highest[..., None]).astype(jnp.bfloat16)
    totals = lax.optimization_barrier(jnp.sum(weights.astype(jnp.float32), axis=-1))
    weighted = jnp.einsum('rhk,rkd->rhd', weights.astype(jnp.float32), values)
    return (highest, totals, weighted)

def join_parts(first, second):
    highest = jnp.maximum(first[0], second[0])
    scale_first = jnp.exp(first[0] - highest)
    scale_second = jnp.exp(second[0] - highest)
    totals = first[1] * scale_first + second[1] * scale_second
    weighted = first[2] * scale_first[..., None] + second[2] * scale_second[..., None]
    return (highest, totals, weighted)

def feed_forward(mlp_in, w_gate, w_up, w_down):
    gate = jnp.dot(mlp_in, w_gate, preferred_element_type=jnp.float32)
    upward = jnp.dot(mlp_in, w_up, preferred_element_type=jnp.float32)
    hidden = (jax.nn.gelu(gate, approximate=True) * upward).astype(jnp.bfloat16)
    return jnp.dot(hidden, w_down, preferred_element_type=jnp.float32)

def reference(x_steps, lengths, perm, parents, table, pool, norm_attn, w_query, w_keyval, w_out, norm_mlp, w_gate, w_up, w_down):
    steps, total_rows, width = x_steps.shape
    head_dim = pool.shape[2] // 2
    heads = w_query.shape[1] // head_dim
    span = table.shape[1] * PAGE
    halves = N_KV // BEAMS
    row_ids = jnp.arange(total_rows, dtype=jnp.int32)
    column = row_ids // RQH
    offset = row_ids % RQH
    member = column % N_KV
    part_of = member // 2 % halves
    beam = member % 2 + 2 * (member // (2 * halves))
    slot = (column // N_KV * halves + part_of) * RQH + offset
    request = perm[slot]
    arrival = (request // RQ * N_KV + member_of(beam, request % RQ // RQH, halves)) * RQH + request % RQH
    inputs = x_steps[:, arrival]
    length = lengths[request]
    first_page = jnp.maximum(length - WINDOW + 1, 0) // PAGE
    key_pos = first_page[:, None] * PAGE + jnp.arange(span, dtype=jnp.int32)[None, :]
    base_columns = column - member
    cache_row = row_ids
    recent = jnp.zeros((total_rows, steps, 2 * head_dim), jnp.bfloat16)
    blocks = total_rows // RQH
    results = []
    for step_index in range(steps):
        parent_rows = (base_columns + member_of(parents[step_index], part_of, halves)) * RQH + offset
        cache_row = cache_row[parent_rows]
        recent = recent[parent_rows]
        current = inputs[step_index]
        normed = rms_round(current, norm_attn)
        query = jnp.dot(normed, w_query, preferred_element_type=jnp.float32).astype(jnp.bfloat16)
        fresh = jnp.dot(normed, w_keyval, preferred_element_type=jnp.float32).astype(jnp.bfloat16)
        recent = recent.at[:, step_index].set(fresh)
        queries = query.reshape(total_rows, heads, head_dim)

        def one_block(packed, step_index=step_index):
            block_queries, block_rows, block_pos, block_length = packed
            block_pages = pool[table[block_rows]].reshape(RQH, span, 2 * head_dim)
            return page_partial(block_queries, block_pages, block_pos, block_length, step_index)
        page = lax.map(one_block, (queries.reshape(blocks, RQH, heads, head_dim), cache_row.reshape(blocks, RQH), key_pos.reshape(blocks, RQH, span), length.reshape(blocks, RQH)))
        page = tuple((part.reshape((total_rows,) + part.shape[2:]) for part in page))
        joined = join_parts(page, fresh_partial(queries, recent, step_index + 1))
        attended = (joined[2] / joined[1][..., None]).astype(jnp.bfloat16).reshape(total_rows, heads * head_dim)
        residual = (current.astype(jnp.float32) + jnp.dot(attended, w_out, preferred_element_type=jnp.float32)).astype(jnp.bfloat16)
        summed = feed_forward(rms_round(residual, norm_mlp), w_gate, w_up, w_down)
        results.append((residual.astype(jnp.float32) + summed).astype(jnp.bfloat16))
    stacked = jnp.stack(results)
    return jnp.zeros_like(stacked).at[:, arrival].set(stacked)
```

```python
import functools

import jax
import jax.numpy as jnp
from jax import lax
from jax.experimental import pallas as pl
from jax.experimental.pallas import tpu as pltpu
from jax.sharding import PartitionSpec as P

WINDOW = 1024
PAGE = 128
BEAMS = 8


EPSILON = 1e-06
NEGATIVE = -1e30


def rms_round(values, gain):
    wide = values.astype(jnp.float32)
    mean_square = jnp.mean(wide * wide, axis=-1, keepdims=True)
    return (wide * lax.rsqrt(mean_square + EPSILON) * gain).astype(jnp.bfloat16)


def feed_forward(mlp_in, w_gate, w_up, w_down):
    gate = jnp.dot(mlp_in, w_gate, preferred_element_type=jnp.float32)
    upward = jnp.dot(mlp_in, w_up, preferred_element_type=jnp.float32)
    hidden = (jax.nn.gelu(gate, approximate=True) * upward).astype(jnp.bfloat16)
    return jnp.dot(hidden, w_down, preferred_element_type=jnp.float32)


def rank_within(labels, offsets):
    earlier = (labels[None, :] == labels[:, None]) & (offsets[None, :] < offsets[:, None])
    return jnp.sum(earlier.astype(jnp.int32), axis=1)


def pick_half(array, halves, half):
    if halves == 1:
        return array
    shaped = array.reshape((BEAMS // 2, halves, 2) + array.shape[1:])
    picked = lax.dynamic_index_in_dim(shaped, half, 1, keepdims=False)
    return picked.reshape((BEAMS,) + array.shape[1:])


def place_block(block, halves, half):
    if halves == 1:
        return block
    whole = jnp.zeros((BEAMS // 2, halves, 2) + block.shape[1:], block.dtype)
    placed = lax.dynamic_update_slice_in_dim(
        whole, block.reshape((BEAMS // 2, 1, 2) + block.shape[1:]), half, 1
    )
    return placed.reshape((BEAMS * halves,) + block.shape[1:])


def exchange(array, axis):
    return lax.all_to_all(array, axis, split_axis=0, concat_axis=0, tiled=True)


def gathered(block, axis):
    count = lax.axis_size(axis)
    return exchange(jnp.broadcast_to(block[None], (count,) + block.shape), axis)


def reordered(selector, array):
    return jnp.einsum(
        "pi,tiw->tpw", selector.astype(jnp.bfloat16), array, preferred_element_type=jnp.float32
    ).astype(jnp.bfloat16)


def attention_kernel(page_count, entries, table_ref, length_ref, *refs):
    pages = refs[:page_count]
    q_ref, new_ref, mask_ref, out_ref = refs[page_count:]
    row = pl.program_id(0)
    length = length_ref[row]
    head_dim = q_ref.shape[-1]
    span = page_count * PAGE
    queries = q_ref[0]
    marks = mask_ref[0].astype(jnp.float32)
    bias = marks[:, :entries]
    held = marks[:, entries : entries + 1]
    step = marks[:, entries + 1 : entries + 2].astype(jnp.int32)
    keys = jnp.concatenate([page[0, :, :head_dim] for page in pages], axis=0)
    values = jnp.concatenate([page[0, :, head_dim:] for page in pages], axis=0)
    first = jnp.maximum(length - WINDOW + 1, 0) // PAGE * PAGE
    shifted = lax.broadcasted_iota(jnp.int32, (1, span), 1) + (first - length + WINDOW)
    contract = (((1,), (1,)), ((), ()))
    scale = head_dim ** (-0.5)
    scores = lax.dot_general(queries, keys, contract, preferred_element_type=jnp.float32) * scale
    scores = jnp.where((shifted < WINDOW) & (shifted > step), scores, NEGATIVE)
    fresh = (
        lax.dot_general(
            queries, new_ref[0, :, :head_dim], contract, preferred_element_type=jnp.float32
        )
        * scale
    )
    fresh = jnp.where(bias > 0.5, fresh, NEGATIVE)
    highest = jnp.maximum(
        jnp.max(scores, axis=-1, keepdims=True), jnp.max(fresh, axis=-1, keepdims=True)
    )
    weights = jnp.exp(scores - highest).astype(jnp.bfloat16)
    fresh_weights = jnp.exp(fresh - highest).astype(jnp.bfloat16)
    totals = jnp.sum(weights.astype(jnp.float32), axis=-1, keepdims=True) + jnp.sum(
        fresh_weights.astype(jnp.float32), axis=-1, keepdims=True
    )
    weighted = jnp.dot(weights, values, preferred_element_type=jnp.float32) + jnp.dot(
        fresh_weights, new_ref[0, :, head_dim:], preferred_element_type=jnp.float32
    )
    out_ref[0] = jnp.where(held > 0.5, weighted / totals, 0.0).astype(jnp.bfloat16)


def attend(local_table, length, pool, queries, entries, marks):
    rows, count, head_dim = queries.shape
    page_count = local_table.shape[1]

    def page_spec(index):
        return pl.BlockSpec(
            (1, PAGE, 2 * head_dim),
            lambda row, table_ref, length_ref: (table_ref[row * page_count + index], 0, 0),
        )

    def row_spec(shape):
        return pl.BlockSpec((1,) + shape[1:], lambda row, table_ref, length_ref: (row, 0, 0))

    return pl.pallas_call(
        functools.partial(attention_kernel, page_count, entries.shape[1]),
        out_shape=jax.ShapeDtypeStruct((rows, count, head_dim), jnp.bfloat16),
        grid_spec=pltpu.PrefetchScalarGridSpec(
            num_scalar_prefetch=2,
            grid=(rows,),
            in_specs=[page_spec(index) for index in range(page_count)]
            + [row_spec(queries.shape), row_spec(entries.shape), row_spec(marks.shape)],
            out_specs=row_spec(queries.shape),
        ),
        compiler_params=pltpu.CompilerParams(vmem_limit_bytes=40 * 2**20),
    )(local_table.reshape(-1), length, *([pool] * page_count), queries, entries, marks)


def on_device(
    x_steps,
    lengths,
    perm,
    parents,
    table,
    pool,
    norm_attn,
    w_query,
    w_keyval,
    w_out,
    norm_mlp,
    w_gate,
    w_up,
    w_down,
):
    steps, rows, width = x_steps.shape
    head_dim = pool.shape[2] // 2
    heads = w_query.shape[1] // head_dim
    req_count = lax.axis_size("req")
    kv_count = lax.axis_size("kv")
    group = lax.axis_index("req")
    member = lax.axis_index("kv")
    halves = kv_count // BEAMS
    half = member // 2 % halves
    beam = member % 2 + 2 * (member // (2 * halves))
    per_group = halves * rows
    group_rows = kv_count * rows
    quota = rows // req_count
    offsets = jnp.arange(rows, dtype=jnp.int32)
    slot_ids = group * per_group + half * rows + offsets
    placed = lax.dynamic_slice_in_dim(perm.reshape(req_count, per_group), half * rows, rows, 1)
    serving = lax.dynamic_index_in_dim(placed, group, 0, keepdims=False)
    target = jnp.sum(
        jnp.where(placed == slot_ids[None, :], jnp.arange(req_count, dtype=jnp.int32)[:, None], 0),
        axis=0,
    )
    anchor = serving // per_group
    to_target = target * quota + rank_within(target, offsets)
    to_anchor = anchor * quota + rank_within(anchor, offsets)
    by_target = to_target[:, None] == offsets[None, :]
    by_anchor = to_anchor[:, None] == offsets[None, :]

    def swap(array):
        shaped = array.reshape(steps, req_count, quota, width)
        return lax.all_to_all(shaped, "req", split_axis=1, concat_axis=1, tiled=True).reshape(
            steps, rows, width
        )

    inputs = reordered(by_anchor, swap(reordered(by_target.T, x_steps)))
    current = inputs.reshape(steps * rows, width)
    length = lengths[serving]
    device = group * kv_count + member

    family = lax.dynamic_slice_in_dim(parents, group * group_rows, group_rows, 1)
    family = family.reshape(steps, kv_count, rows).transpose(1, 0, 2)
    family = pick_half(family, halves, half)
    beams = jnp.arange(BEAMS, dtype=jnp.int32)
    own = jnp.broadcast_to(beams[:, None], (BEAMS, rows))
    origins = [own]
    tables = []
    for step_index in range(steps):
        chosen = family[:, step_index][:, None, :] == beams[None, :, None]
        origins = [jnp.sum(jnp.where(chosen, origin[None], 0), axis=1) for origin in origins]
        origins.append(own)
        tables.append(
            jnp.stack(origins + [jnp.full_like(own, -1)] * (steps - 1 - step_index))
        )
    lineage = jnp.stack(tables)
    held = (lineage[:, 0] == beam).transpose(2, 1, 0)
    linked = lineage[:, 1:, :, :, None] == beams
    linked = linked.transpose(3, 2, 0, 4, 1).reshape(rows, BEAMS * steps, BEAMS * steps)
    step_marks = jnp.broadcast_to(
        jnp.arange(steps, dtype=jnp.int32), (rows, BEAMS, steps)
    )
    marks = jnp.concatenate(
        [
            linked.astype(jnp.bfloat16),
            held.reshape(rows, BEAMS * steps, 1).astype(jnp.bfloat16),
            step_marks.reshape(rows, BEAMS * steps, 1).astype(jnp.bfloat16),
        ],
        axis=2,
    )
    mark_count = marks.shape[2]
    marks = jnp.broadcast_to(
        marks[:, :, None, :], (rows, BEAMS * steps, heads, mark_count)
    ).reshape(rows, BEAMS * steps * heads, mark_count)

    normed = rms_round(current, norm_attn)
    query = jnp.dot(normed, w_query, preferred_element_type=jnp.float32).astype(jnp.bfloat16)
    fresh = jnp.dot(normed, w_keyval, preferred_element_type=jnp.float32).astype(jnp.bfloat16)
    sent = jnp.concatenate([query, fresh], axis=1)
    shared = pick_half(gathered(sent, "kv"), halves, half)
    shared = shared.reshape(BEAMS, steps, rows, -1).transpose(2, 0, 1, 3)
    queries = shared[..., : heads * head_dim].reshape(rows, BEAMS * steps * heads, head_dim)
    entries = shared[..., heads * head_dim :].reshape(rows, BEAMS * steps, 2 * head_dim)
    answers = attend(
        table - device * pool.shape[0], length, pool, queries, entries, marks
    )
    answers = answers.reshape(rows, BEAMS, steps, heads * head_dim).transpose(1, 2, 0, 3)
    returned = exchange(
        place_block(answers.reshape(BEAMS, steps * rows, heads * head_dim), halves, half), "kv"
    )
    attended = jnp.sum(returned.astype(jnp.float32), axis=0).astype(jnp.bfloat16)
    residual = (
        current.astype(jnp.float32) + jnp.dot(attended, w_out, preferred_element_type=jnp.float32)
    ).astype(jnp.bfloat16)
    everyone = gathered(rms_round(residual, norm_mlp), "kv").reshape(-1, width)
    terms = feed_forward(everyone, w_gate, w_up, w_down).astype(jnp.bfloat16)
    terms = exchange(terms.reshape(kv_count, steps * rows, width), "kv")
    summed = jnp.sum(terms.astype(jnp.float32), axis=0)
    finished = (residual.astype(jnp.float32) + summed).astype(jnp.bfloat16)
    finished = finished.reshape(steps, rows, width)
    return reordered(by_target, swap(reordered(by_anchor.T, finished)))


def solution(mesh):
    in_specs = (
        P(None, ("req", "kv"), None),
        P(),
        P(),
        P(),
        P(("req", "kv"), None),
        P(("req", "kv"), None, None),
        P(),
        P(),
        P(),
        P(),
        P(),
        P(None, "kv"),
        P(None, "kv"),
        P("kv", None),
    )
    out_specs = P(None, ("req", "kv"), None)
    return jax.shard_map(
        on_device, mesh=mesh, in_specs=in_specs, out_specs=out_specs, check_vma=False
    )
```

```python
import functools

import jax
import jax.numpy as jnp
from jax import lax
from jax.experimental import pallas as pl
from jax.experimental.pallas import tpu as pltpu
from jax.sharding import PartitionSpec as P

WINDOW = 1024
PAGE = 128
BEAMS = 8


EPSILON = 1e-06
NEGATIVE = -1e30


def rms_round(values, gain):
    wide = values.astype(jnp.float32)
    mean_square = jnp.mean(wide * wide, axis=-1, keepdims=True)
    return (wide * lax.rsqrt(mean_square + EPSILON) * gain).astype(jnp.bfloat16)


def feed_forward(mlp_in, w_gate, w_up, w_down):
    gate = jnp.dot(mlp_in, w_gate, preferred_element_type=jnp.float32)
    upward = jnp.dot(mlp_in, w_up, preferred_element_type=jnp.float32)
    hidden = (jax.nn.gelu(gate, approximate=True) * upward).astype(jnp.bfloat16)
    return jnp.dot(hidden, w_down, preferred_element_type=jnp.float32)


def rank_within(labels, offsets):
    earlier = (labels[None, :] == labels[:, None]) & (offsets[None, :] < offsets[:, None])
    return jnp.sum(earlier.astype(jnp.int32), axis=1)


def pick_half(array, halves, half):
    if halves == 1:
        return array
    shaped = array.reshape((BEAMS // 2, halves, 2) + array.shape[1:])
    picked = lax.dynamic_index_in_dim(shaped, half, 1, keepdims=False)
    return picked.reshape((BEAMS,) + array.shape[1:])


def place_block(block, halves, half):
    if halves == 1:
        return block
    whole = jnp.zeros((BEAMS // 2, halves, 2) + block.shape[1:], block.dtype)
    placed = lax.dynamic_update_slice_in_dim(
        whole, block.reshape((BEAMS // 2, 1, 2) + block.shape[1:]), half, 1
    )
    return placed.reshape((BEAMS * halves,) + block.shape[1:])


MESH = pl.DeviceIdType.MESH


class Sends:
    def __init__(self, send_sem):
        self.send_sem = send_sem
        self.started = []

    def go(self, where, source, target, arrived, peer):
        copy = pltpu.make_async_remote_copy(
            src_ref=source,
            dst_ref=target,
            send_sem=self.send_sem.at[len(self.started)],
            recv_sem=arrived,
            device_id={"kv": peer},
            device_id_type=MESH,
        )
        self.started.append((where, copy))
        if where is None:
            copy.start()
        else:
            pl.when(where)(copy.start)

    def finish(self):
        for where, copy in self.started:
            if where is None:
                copy.wait_send()
            else:
                pl.when(where)(copy.wait_send)


def landed(where, target, arrived):
    def wait():
        pltpu.make_async_copy(target, target, arrived).wait()

    if where is None:
        wait()
    else:
        pl.when(where)(wait)


def place_on_lines(count):
    me = lax.axis_index("kv")
    low = lax.rem(me, 2)
    high = me // 2
    length = count // 2
    above, below = high + 1 < length, high > 0
    partner = high * 2 + 1 - low
    up = jnp.minimum(high + 1, length - 1) * 2 + low
    down = jnp.maximum(high - 1, 0) * 2 + low
    return me, low, high, length, above, below, partner, up, down


def greet(above, below, partner, up, down):
    barrier = pltpu.get_barrier_semaphore()

    def hello(peer):
        pl.semaphore_signal(barrier, inc=1, device_id={"kv": peer}, device_id_type=MESH)

    hello(partner)
    pl.when(above)(lambda: hello(up))
    pl.when(below)(lambda: hello(down))
    pl.semaphore_wait(barrier, 1 + above.astype(jnp.int32) + below.astype(jnp.int32))


def gather_kernel(count, own_ref, all_ref, send_sem, first_sem, second_sem):
    me, low, high, length, above, below, partner, up, down = place_on_lines(count)
    middle = own_ref.shape[0] // 2
    first, second = pl.ds(0, middle), pl.ds(middle, middle)
    greet(above, below, partner, up, down)
    sends = Sends(send_sem)

    def spread(where, block, source, part, sems, peer):
        sends.go(where, source, all_ref.at[block, part], sems.at[block], peer)

    spread(None, me, own_ref.at[second], second, second_sem, partner)
    for where, peer in ((above, up), (below, down)):
        spread(where, me, own_ref.at[first], first, first_sem, peer)
        spread(where, me, own_ref.at[second], second, second_sem, peer)
    spread(None, me, own_ref.at[first], first, first_sem, partner)
    all_ref[me] = own_ref[...]
    landed(None, all_ref.at[partner, second], second_sem.at[partner])
    for where, peer in ((above, up), (below, down)):
        spread(where, partner, all_ref.at[partner, second], second, second_sem, peer)
    for distance in range(1, length):
        for source, here, where, peer in (
            (jnp.maximum(high - distance, 0), high >= distance, above, up),
            (jnp.minimum(high + distance, length - 1), high + distance < length, below, down),
        ):
            same = source * 2 + low
            cross = source * 2 + 1 - low
            onward = here & where
            landed(here, all_ref.at[same, first], first_sem.at[same])
            spread(onward, same, all_ref.at[same, first], first, first_sem, peer)
            spread(here, same, all_ref.at[same, first], first, first_sem, partner)
            landed(here, all_ref.at[same, second], second_sem.at[same])
            spread(onward, same, all_ref.at[same, second], second, second_sem, peer)
            landed(here, all_ref.at[cross, second], second_sem.at[cross])
            spread(onward, cross, all_ref.at[cross, second], second, second_sem, peer)
    for line in range(length):
        cross = line * 2 + 1 - low
        landed(None, all_ref.at[cross, first], first_sem.at[cross])
    sends.finish()


def gathered(block, count, collective_id):
    whole = pl.BlockSpec(memory_space=pltpu.VMEM)
    return pl.pallas_call(
        functools.partial(gather_kernel, count),
        out_shape=jax.ShapeDtypeStruct((count,) + block.shape, block.dtype),
        in_specs=[whole],
        out_specs=whole,
        scratch_shapes=[
            pltpu.SemaphoreType.DMA((8 + 10 * (count // 2),)),
            pltpu.SemaphoreType.DMA((count,)),
            pltpu.SemaphoreType.DMA((count,)),
        ],
        compiler_params=pltpu.CompilerParams(
            collective_id=collective_id, has_side_effects=True, vmem_limit_bytes=40 * 2**20
        ),
    )(block)


def reduce_kernel(
    count,
    terms_ref,
    sum_ref,
    cross_first,
    up_first,
    down_first,
    stage_first,
    cross_second,
    up_second,
    down_second,
    stage_second,
    stage_cross,
    send_sem,
    cross_sem,
    up_sem,
    down_sem,
):
    me, low, high, length, above, below, partner, up, down = place_on_lines(count)
    middle = sum_ref.shape[0] // 2
    first, second = pl.ds(0, middle), pl.ds(middle, middle)
    greet(above, below, partner, up, down)
    sends = Sends(send_sem)
    for line in range(length):
        sends.go(
            None,
            terms_ref.at[line * 2 + 1 - low, first],
            cross_first.at[line],
            cross_sem.at[line],
            partner,
        )

    def wide(ref):
        return ref[...].astype(jnp.float32)

    def base_first(line):
        return wide(terms_ref.at[line * 2 + low, first]) + wide(cross_first.at[line])

    def pass_on(here, line, behind, slot, stage, arrived, ahead, base):
        def with_slot():
            stage[...] = (base() + wide(slot)).astype(stage.dtype)

        def alone():
            stage[...] = base().astype(stage.dtype)

        landed(here & behind, slot, arrived)
        pl.when(here & behind)(with_slot)
        pl.when(here & jnp.logical_not(behind))(alone)
        sends.go(here, stage, slot, arrived, ahead)

    directions = (
        (1, below, up_second, up_first, up_sem, up),
        (-1, above, down_second, down_first, down_sem, down),
    )
    for distance in range(length - 1, 0, -1):
        for sign, behind, slot, _, sems, ahead in directions:
            line = high + sign * distance
            here = (line < length) & (line >= 0)
            line = jnp.clip(line, 0, length - 1)
            for other in range(2):
                side = low if other == 0 else 1 - low
                block = line * 2 + side
                pass_on(
                    here,
                    line,
                    behind,
                    slot.at[block],
                    stage_second.at[block],
                    sems.at[length + block],
                    ahead,
                    lambda block=block: wide(terms_ref.at[block, second]),
                )
    for line in range(length):
        landed(None, cross_first.at[line], cross_sem.at[line])
    for distance in range(length - 1, 0, -1):
        for sign, behind, _, slot, sems, ahead in directions:
            line = high + sign * distance
            here = (line < length) & (line >= 0)
            line = jnp.clip(line, 0, length - 1)
            pass_on(
                here,
                line,
                behind,
                slot.at[line],
                stage_first.at[line],
                sems.at[line],
                ahead,
                lambda line=line: base_first(line),
            )

    def collect(into, part, value, up_slot, down_slot, up_arrived, down_arrived):
        into[part, :] = value
        landed(below, up_slot, up_arrived)
        landed(above, down_slot, down_arrived)

        def add(slot):
            into[part, :] += wide(slot)

        pl.when(below)(lambda: add(up_slot))
        pl.when(above)(lambda: add(down_slot))

    collect(
        sum_ref,
        second,
        wide(terms_ref.at[partner, second]),
        up_second.at[partner],
        down_second.at[partner],
        up_sem.at[length + partner],
        down_sem.at[length + partner],
    )
    stage_cross[...] = sum_ref[second, :].astype(stage_cross.dtype)
    sends.go(None, stage_cross, cross_second, cross_sem.at[length], partner)
    collect(
        sum_ref,
        second,
        wide(terms_ref.at[me, second]),
        up_second.at[me],
        down_second.at[me],
        up_sem.at[length + me],
        down_sem.at[length + me],
    )
    collect(
        sum_ref,
        first,
        base_first(high),
        up_first.at[high],
        down_first.at[high],
        up_sem.at[high],
        down_sem.at[high],
    )
    landed(None, cross_second, cross_sem.at[length])
    sum_ref[second, :] += wide(cross_second)
    sends.finish()


def reduced(terms, collective_id):
    count, rows, width = terms.shape
    length = count // 2
    whole = pl.BlockSpec(memory_space=pltpu.VMEM)

    def slots(*shape):
        return pltpu.VMEM(shape + (rows // 2, width), terms.dtype)

    return pl.pallas_call(
        functools.partial(reduce_kernel, count),
        out_shape=jax.ShapeDtypeStruct((rows, width), jnp.float32),
        in_specs=[whole],
        out_specs=whole,
        scratch_shapes=[
            slots(length),
            slots(length),
            slots(length),
            slots(length),
            slots(),
            slots(count),
            slots(count),
            slots(count),
            slots(),
            pltpu.SemaphoreType.DMA((8 * length,)),
            pltpu.SemaphoreType.DMA((length + 1,)),
            pltpu.SemaphoreType.DMA((length + count,)),
            pltpu.SemaphoreType.DMA((length + count,)),
        ],
        compiler_params=pltpu.CompilerParams(
            collective_id=collective_id, has_side_effects=True, vmem_limit_bytes=40 * 2**20
        ),
    )(terms)


def reordered(selector, array):
    return jnp.einsum(
        "pi,tiw->tpw", selector.astype(jnp.bfloat16), array, preferred_element_type=jnp.float32
    ).astype(jnp.bfloat16)


def attention_kernel(page_count, entries, table_ref, length_ref, *refs):
    pages = refs[:page_count]
    q_ref, new_ref, mask_ref, out_ref = refs[page_count:]
    row = pl.program_id(0)
    length = length_ref[row]
    head_dim = q_ref.shape[-1]
    span = page_count * PAGE
    queries = q_ref[0]
    marks = mask_ref[0].astype(jnp.float32)
    bias = marks[:, :entries]
    held = marks[:, entries : entries + 1]
    step = marks[:, entries + 1 : entries + 2].astype(jnp.int32)
    keys = jnp.concatenate([page[0, :, :head_dim] for page in pages], axis=0)
    values = jnp.concatenate([page[0, :, head_dim:] for page in pages], axis=0)
    first = jnp.maximum(length - WINDOW + 1, 0) // PAGE * PAGE
    shifted = lax.broadcasted_iota(jnp.int32, (1, span), 1) + (first - length + WINDOW)
    contract = (((1,), (1,)), ((), ()))
    scale = head_dim ** (-0.5)
    scores = lax.dot_general(queries, keys, contract, preferred_element_type=jnp.float32) * scale
    scores = jnp.where((shifted < WINDOW) & (shifted > step), scores, NEGATIVE)
    fresh = (
        lax.dot_general(
            queries, new_ref[0, :, :head_dim], contract, preferred_element_type=jnp.float32
        )
        * scale
    )
    fresh = jnp.where(bias > 0.5, fresh, NEGATIVE)
    highest = jnp.maximum(
        jnp.max(scores, axis=-1, keepdims=True), jnp.max(fresh, axis=-1, keepdims=True)
    )
    weights = jnp.exp(scores - highest).astype(jnp.bfloat16)
    fresh_weights = jnp.exp(fresh - highest).astype(jnp.bfloat16)
    totals = jnp.sum(weights.astype(jnp.float32), axis=-1, keepdims=True) + jnp.sum(
        fresh_weights.astype(jnp.float32), axis=-1, keepdims=True
    )
    weighted = jnp.dot(weights, values, preferred_element_type=jnp.float32) + jnp.dot(
        fresh_weights, new_ref[0, :, head_dim:], preferred_element_type=jnp.float32
    )
    out_ref[0] = jnp.where(held > 0.5, weighted / totals, 0.0).astype(jnp.bfloat16)


def attend(local_table, length, pool, queries, entries, marks):
    rows, count, head_dim = queries.shape
    page_count = local_table.shape[1]

    def page_spec(index):
        return pl.BlockSpec(
            (1, PAGE, 2 * head_dim),
            lambda row, table_ref, length_ref: (table_ref[row * page_count + index], 0, 0),
        )

    def row_spec(shape):
        return pl.BlockSpec((1,) + shape[1:], lambda row, table_ref, length_ref: (row, 0, 0))

    return pl.pallas_call(
        functools.partial(attention_kernel, page_count, entries.shape[1]),
        out_shape=jax.ShapeDtypeStruct((rows, count, head_dim), jnp.bfloat16),
        grid_spec=pltpu.PrefetchScalarGridSpec(
            num_scalar_prefetch=2,
            grid=(rows,),
            in_specs=[page_spec(index) for index in range(page_count)]
            + [row_spec(queries.shape), row_spec(entries.shape), row_spec(marks.shape)],
            out_specs=row_spec(queries.shape),
        ),
        compiler_params=pltpu.CompilerParams(vmem_limit_bytes=40 * 2**20),
    )(local_table.reshape(-1), length, *([pool] * page_count), queries, entries, marks)


def on_device(
    x_steps,
    lengths,
    perm,
    parents,
    table,
    pool,
    norm_attn,
    w_query,
    w_keyval,
    w_out,
    norm_mlp,
    w_gate,
    w_up,
    w_down,
):
    steps, rows, width = x_steps.shape
    head_dim = pool.shape[2] // 2
    heads = w_query.shape[1] // head_dim
    req_count = lax.axis_size("req")
    kv_count = lax.axis_size("kv")
    group = lax.axis_index("req")
    member = lax.axis_index("kv")
    halves = kv_count // BEAMS
    half = member // 2 % halves
    beam = member % 2 + 2 * (member // (2 * halves))
    per_group = halves * rows
    group_rows = kv_count * rows
    quota = rows // req_count
    offsets = jnp.arange(rows, dtype=jnp.int32)
    slot_ids = group * per_group + half * rows + offsets
    placed = lax.dynamic_slice_in_dim(perm.reshape(req_count, per_group), half * rows, rows, 1)
    serving = lax.dynamic_index_in_dim(placed, group, 0, keepdims=False)
    target = jnp.sum(
        jnp.where(placed == slot_ids[None, :], jnp.arange(req_count, dtype=jnp.int32)[:, None], 0),
        axis=0,
    )
    anchor = serving // per_group
    to_target = target * quota + rank_within(target, offsets)
    to_anchor = anchor * quota + rank_within(anchor, offsets)
    by_target = to_target[:, None] == offsets[None, :]
    by_anchor = to_anchor[:, None] == offsets[None, :]

    def swap(array):
        shaped = array.reshape(steps, req_count, quota, width)
        return lax.all_to_all(shaped, "req", split_axis=1, concat_axis=1, tiled=True).reshape(
            steps, rows, width
        )

    inputs = reordered(by_anchor, swap(reordered(by_target.T, x_steps)))
    current = inputs.reshape(steps * rows, width)
    length = lengths[serving]
    device = group * kv_count + member

    family = lax.dynamic_slice_in_dim(parents, group * group_rows, group_rows, 1)
    family = family.reshape(steps, kv_count, rows).transpose(1, 0, 2)
    family = pick_half(family, halves, half)
    beams = jnp.arange(BEAMS, dtype=jnp.int32)
    own = jnp.broadcast_to(beams[:, None], (BEAMS, rows))
    origins = [own]
    tables = []
    for step_index in range(steps):
        chosen = family[:, step_index][:, None, :] == beams[None, :, None]
        origins = [jnp.sum(jnp.where(chosen, origin[None], 0), axis=1) for origin in origins]
        origins.append(own)
        tables.append(
            jnp.stack(origins + [jnp.full_like(own, -1)] * (steps - 1 - step_index))
        )
    lineage = jnp.stack(tables)
    held = (lineage[:, 0] == beam).transpose(2, 1, 0)
    linked = lineage[:, 1:, :, :, None] == beams
    linked = linked.transpose(3, 2, 0, 4, 1).reshape(rows, BEAMS * steps, BEAMS * steps)
    step_marks = jnp.broadcast_to(
        jnp.arange(steps, dtype=jnp.int32), (rows, BEAMS, steps)
    )
    marks = jnp.concatenate(
        [
            linked.astype(jnp.bfloat16),
            held.reshape(rows, BEAMS * steps, 1).astype(jnp.bfloat16),
            step_marks.reshape(rows, BEAMS * steps, 1).astype(jnp.bfloat16),
        ],
        axis=2,
    )
    mark_count = marks.shape[2]
    marks = jnp.broadcast_to(
        marks[:, :, None, :], (rows, BEAMS * steps, heads, mark_count)
    ).reshape(rows, BEAMS * steps * heads, mark_count)

    normed = rms_round(current, norm_attn)
    query = jnp.dot(normed, w_query, preferred_element_type=jnp.float32).astype(jnp.bfloat16)
    fresh = jnp.dot(normed, w_keyval, preferred_element_type=jnp.float32).astype(jnp.bfloat16)
    sent = jnp.concatenate([query, fresh], axis=1)
    shared = pick_half(gathered(sent, kv_count, 1), halves, half)
    shared = shared.reshape(BEAMS, steps, rows, -1).transpose(2, 0, 1, 3)
    queries = shared[..., : heads * head_dim].reshape(rows, BEAMS * steps * heads, head_dim)
    entries = shared[..., heads * head_dim :].reshape(rows, BEAMS * steps, 2 * head_dim)
    answers = attend(
        table - device * pool.shape[0], length, pool, queries, entries, marks
    )
    answers = answers.reshape(rows, BEAMS, steps, heads * head_dim).transpose(1, 2, 0, 3)
    attended = reduced(
        place_block(answers.reshape(BEAMS, steps * rows, heads * head_dim), halves, half), 2
    ).astype(jnp.bfloat16)
    residual = (
        current.astype(jnp.float32) + jnp.dot(attended, w_out, preferred_element_type=jnp.float32)
    ).astype(jnp.bfloat16)
    everyone = gathered(rms_round(residual, norm_mlp), kv_count, 3).reshape(-1, width)
    terms = feed_forward(everyone, w_gate, w_up, w_down).astype(jnp.bfloat16)
    summed = reduced(terms.reshape(kv_count, steps * rows, width), 4)
    finished = (residual.astype(jnp.float32) + summed).astype(jnp.bfloat16)
    finished = finished.reshape(steps, rows, width)
    return reordered(by_target, swap(reordered(by_anchor.T, finished)))


def solution(mesh):
    in_specs = (
        P(None, ("req", "kv"), None),
        P(),
        P(),
        P(),
        P(("req", "kv"), None),
        P(("req", "kv"), None, None),
        P(),
        P(),
        P(),
        P(),
        P(),
        P(None, "kv"),
        P(None, "kv"),
        P("kv", None),
    )
    out_specs = P(None, ("req", "kv"), None)
    return jax.shard_map(
        on_device, mesh=mesh, in_specs=in_specs, out_specs=out_specs, check_vma=False
    )
```

```python
import functools

import jax
import jax.numpy as jnp
from jax import lax
from jax.experimental import pallas as pl
from jax.experimental.pallas import tpu as pltpu
from jax.sharding import PartitionSpec as P

WINDOW = 1024
PAGE = 128
BEAMS = 8


EPSILON = 1e-06
NEGATIVE = -1e30


def rms_round(values, gain):
    wide = values.astype(jnp.float32)
    mean_square = jnp.mean(wide * wide, axis=-1, keepdims=True)
    return (wide * lax.rsqrt(mean_square + EPSILON) * gain).astype(jnp.bfloat16)


def feed_forward(mlp_in, w_gate, w_up, w_down):
    gate = jnp.dot(mlp_in, w_gate, preferred_element_type=jnp.float32)
    upward = jnp.dot(mlp_in, w_up, preferred_element_type=jnp.float32)
    hidden = (jax.nn.gelu(gate, approximate=True) * upward).astype(jnp.bfloat16)
    return jnp.dot(hidden, w_down, preferred_element_type=jnp.float32)


def rank_within(labels, offsets):
    earlier = (labels[None, :] == labels[:, None]) & (offsets[None, :] < offsets[:, None])
    return jnp.sum(earlier.astype(jnp.int32), axis=1)


def pick_half(array, halves, half):
    if halves == 1:
        return array
    shaped = array.reshape((BEAMS // 2, halves, 2) + array.shape[1:])
    picked = lax.dynamic_index_in_dim(shaped, half, 1, keepdims=False)
    return picked.reshape((BEAMS,) + array.shape[1:])


def place_block(block, halves, half):
    if halves == 1:
        return block
    whole = jnp.zeros((BEAMS // 2, halves, 2) + block.shape[1:], block.dtype)
    placed = lax.dynamic_update_slice_in_dim(
        whole, block.reshape((BEAMS // 2, 1, 2) + block.shape[1:]), half, 1
    )
    return placed.reshape((BEAMS * halves,) + block.shape[1:])


MESH = pl.DeviceIdType.MESH


class Sends:
    def __init__(self, send_sem):
        self.send_sem = send_sem
        self.started = []

    def go(self, where, source, target, arrived, peer):
        copy = pltpu.make_async_remote_copy(
            src_ref=source,
            dst_ref=target,
            send_sem=self.send_sem.at[len(self.started)],
            recv_sem=arrived,
            device_id={"kv": peer},
            device_id_type=MESH,
        )
        self.started.append((where, copy))
        if where is None:
            copy.start()
        else:
            pl.when(where)(copy.start)

    def finish(self):
        for where, copy in self.started:
            if where is None:
                copy.wait_send()
            else:
                pl.when(where)(copy.wait_send)


def landed(where, target, arrived):
    def wait():
        pltpu.make_async_copy(target, target, arrived).wait()

    if where is None:
        wait()
    else:
        pl.when(where)(wait)


def place_on_lines(count):
    me = lax.axis_index("kv")
    low = lax.rem(me, 2)
    high = me // 2
    length = count // 2
    above, below = high + 1 < length, high > 0
    partner = high * 2 + 1 - low
    up = jnp.minimum(high + 1, length - 1) * 2 + low
    down = jnp.maximum(high - 1, 0) * 2 + low
    return me, low, high, length, above, below, partner, up, down


def greet(above, below, partner, up, down):
    barrier = pltpu.get_barrier_semaphore()

    def hello(peer):
        pl.semaphore_signal(barrier, inc=1, device_id={"kv": peer}, device_id_type=MESH)

    hello(partner)
    pl.when(above)(lambda: hello(up))
    pl.when(below)(lambda: hello(down))
    pl.semaphore_wait(barrier, 1 + above.astype(jnp.int32) + below.astype(jnp.int32))


def gather_kernel(count, greeting, own_ref, all_ref, send_sem, first_sem, second_sem):
    me, low, high, length, above, below, partner, up, down = place_on_lines(count)
    middle = own_ref.shape[0] // 2
    first, second = pl.ds(0, middle), pl.ds(middle, middle)
    if greeting:
        greet(above, below, partner, up, down)
    sends = Sends(send_sem)

    def spread(where, block, source, part, sems, peer):
        sends.go(where, source, all_ref.at[block, part], sems.at[block], peer)

    spread(None, me, own_ref.at[second], second, second_sem, partner)
    for where, peer in ((above, up), (below, down)):
        spread(where, me, own_ref.at[first], first, first_sem, peer)
        spread(where, me, own_ref.at[second], second, second_sem, peer)
    spread(None, me, own_ref.at[first], first, first_sem, partner)
    all_ref[me] = own_ref[...]
    landed(None, all_ref.at[partner, second], second_sem.at[partner])
    for where, peer in ((above, up), (below, down)):
        spread(where, partner, all_ref.at[partner, second], second, second_sem, peer)
    for distance in range(1, length):
        for source, here, where, peer in (
            (jnp.maximum(high - distance, 0), high >= distance, above, up),
            (jnp.minimum(high + distance, length - 1), high + distance < length, below, down),
        ):
            same = source * 2 + low
            cross = source * 2 + 1 - low
            onward = here & where
            landed(here, all_ref.at[same, first], first_sem.at[same])
            spread(onward, same, all_ref.at[same, first], first, first_sem, peer)
            spread(here, same, all_ref.at[same, first], first, first_sem, partner)
            landed(here, all_ref.at[same, second], second_sem.at[same])
            spread(onward, same, all_ref.at[same, second], second, second_sem, peer)
            landed(here, all_ref.at[cross, second], second_sem.at[cross])
            spread(onward, cross, all_ref.at[cross, second], second, second_sem, peer)
    for line in range(length):
        cross = line * 2 + 1 - low
        landed(None, all_ref.at[cross, first], first_sem.at[cross])
    sends.finish()


def gathered(block, count, collective_id):
    whole = pl.BlockSpec(memory_space=pltpu.VMEM)
    return pl.pallas_call(
        functools.partial(gather_kernel, count, True),
        out_shape=jax.ShapeDtypeStruct((count,) + block.shape, block.dtype),
        in_specs=[whole],
        out_specs=whole,
        scratch_shapes=gather_semaphores(count),
        compiler_params=pltpu.CompilerParams(
            collective_id=collective_id, has_side_effects=True, vmem_limit_bytes=40 * 2**20
        ),
    )(block)


def reduce_kernel(
    count,
    terms_ref,
    sum_ref,
    cross_first,
    up_first,
    down_first,
    stage_first,
    cross_second,
    up_second,
    down_second,
    stage_second,
    stage_cross,
    send_sem,
    cross_sem,
    up_sem,
    down_sem,
):
    me, low, high, length, above, below, partner, up, down = place_on_lines(count)
    middle = sum_ref.shape[0] // 2
    first, second = pl.ds(0, middle), pl.ds(middle, middle)
    greet(above, below, partner, up, down)
    sends = Sends(send_sem)
    for line in range(length):
        sends.go(
            None,
            terms_ref.at[line * 2 + 1 - low, first],
            cross_first.at[line],
            cross_sem.at[line],
            partner,
        )

    def wide(ref):
        return ref[...].astype(jnp.float32)

    def base_first(line):
        return wide(terms_ref.at[line * 2 + low, first]) + wide(cross_first.at[line])

    def pass_on(here, line, behind, slot, stage, arrived, ahead, base):
        def with_slot():
            stage[...] = (base() + wide(slot)).astype(stage.dtype)

        def alone():
            stage[...] = base().astype(stage.dtype)

        landed(here & behind, slot, arrived)
        pl.when(here & behind)(with_slot)
        pl.when(here & jnp.logical_not(behind))(alone)
        sends.go(here, stage, slot, arrived, ahead)

    directions = (
        (1, below, up_second, up_first, up_sem, up),
        (-1, above, down_second, down_first, down_sem, down),
    )
    for distance in range(length - 1, 0, -1):
        for sign, behind, slot, _, sems, ahead in directions:
            line = high + sign * distance
            here = (line < length) & (line >= 0)
            line = jnp.clip(line, 0, length - 1)
            for other in range(2):
                side = low if other == 0 else 1 - low
                block = line * 2 + side
                pass_on(
                    here,
                    line,
                    behind,
                    slot.at[block],
                    stage_second.at[block],
                    sems.at[length + block],
                    ahead,
                    lambda block=block: wide(terms_ref.at[block, second]),
                )
    for line in range(length):
        landed(None, cross_first.at[line], cross_sem.at[line])
    for distance in range(length - 1, 0, -1):
        for sign, behind, _, slot, sems, ahead in directions:
            line = high + sign * distance
            here = (line < length) & (line >= 0)
            line = jnp.clip(line, 0, length - 1)
            pass_on(
                here,
                line,
                behind,
                slot.at[line],
                stage_first.at[line],
                sems.at[line],
                ahead,
                lambda line=line: base_first(line),
            )

    def collect(into, part, value, up_slot, down_slot, up_arrived, down_arrived):
        into[part, :] = value
        landed(below, up_slot, up_arrived)
        landed(above, down_slot, down_arrived)

        def add(slot):
            into[part, :] += wide(slot)

        pl.when(below)(lambda: add(up_slot))
        pl.when(above)(lambda: add(down_slot))

    collect(
        sum_ref,
        second,
        wide(terms_ref.at[partner, second]),
        up_second.at[partner],
        down_second.at[partner],
        up_sem.at[length + partner],
        down_sem.at[length + partner],
    )
    stage_cross[...] = sum_ref[second, :].astype(stage_cross.dtype)
    sends.go(None, stage_cross, cross_second, cross_sem.at[length], partner)
    collect(
        sum_ref,
        second,
        wide(terms_ref.at[me, second]),
        up_second.at[me],
        down_second.at[me],
        up_sem.at[length + me],
        down_sem.at[length + me],
    )
    collect(
        sum_ref,
        first,
        base_first(high),
        up_first.at[high],
        down_first.at[high],
        up_sem.at[high],
        down_sem.at[high],
    )
    landed(None, cross_second, cross_sem.at[length])
    sum_ref[second, :] += wide(cross_second)
    sends.finish()


def gather_semaphores(count):
    return [
        pltpu.SemaphoreType.DMA((8 + 10 * (count // 2),)),
        pltpu.SemaphoreType.DMA((count,)),
        pltpu.SemaphoreType.DMA((count,)),
    ]


def reduce_scratch(terms):
    count, rows, width = terms.shape
    length = count // 2

    def slots(*shape):
        return pltpu.VMEM(shape + (rows // 2, width), terms.dtype)

    return [
        slots(length),
        slots(length),
        slots(length),
        slots(length),
        slots(),
        slots(count),
        slots(count),
        slots(count),
        slots(),
        pltpu.SemaphoreType.DMA((8 * length,)),
        pltpu.SemaphoreType.DMA((length + 1,)),
        pltpu.SemaphoreType.DMA((length + count,)),
        pltpu.SemaphoreType.DMA((length + count,)),
    ]


def reduced(terms, collective_id):
    count, rows, width = terms.shape
    whole = pl.BlockSpec(memory_space=pltpu.VMEM)
    return pl.pallas_call(
        functools.partial(reduce_kernel, count),
        out_shape=jax.ShapeDtypeStruct((rows, width), jnp.float32),
        in_specs=[whole],
        out_specs=whole,
        scratch_shapes=reduce_scratch(terms),
        compiler_params=pltpu.CompilerParams(
            collective_id=collective_id, has_side_effects=True, vmem_limit_bytes=40 * 2**20
        ),
    )(terms)


def share_kernel(count, terms_ref, all_ref, sum_ref, own_ref, *scratch):
    reduce_kernel(count, terms_ref, sum_ref, *scratch[:-3])
    own_ref[...] = sum_ref[...].astype(own_ref.dtype)
    gather_kernel(count, False, own_ref, all_ref, *scratch[-3:])


def shared_sum(terms, collective_id):
    count, rows, width = terms.shape
    whole = pl.BlockSpec(memory_space=pltpu.VMEM)
    return pl.pallas_call(
        functools.partial(share_kernel, count),
        out_shape=jax.ShapeDtypeStruct(terms.shape, terms.dtype),
        in_specs=[whole],
        out_specs=whole,
        scratch_shapes=[
            pltpu.VMEM((rows, width), jnp.float32),
            pltpu.VMEM((rows, width), terms.dtype),
        ]
        + reduce_scratch(terms)
        + gather_semaphores(count),
        compiler_params=pltpu.CompilerParams(
            collective_id=collective_id, has_side_effects=True, vmem_limit_bytes=40 * 2**20
        ),
    )(terms)


def reordered(selector, array):
    return jnp.einsum(
        "pi,tiw->tpw", selector.astype(jnp.bfloat16), array, preferred_element_type=jnp.float32
    ).astype(jnp.bfloat16)


def attention_kernel(page_count, heads, stride, table_ref, length_ref, *refs):
    pages = refs[:page_count]
    q_ref, new_ref, mask_ref, out_ref, q_heads, new_parts, out_heads = refs[page_count:]
    row = pl.program_id(0)
    length = length_ref[row]
    entries = mask_ref.shape[1]
    head_dim = q_ref.shape[1] // heads
    span = page_count * PAGE
    family = pl.ds(row, entries, stride=stride)

    def columns(part):
        return pl.ds(part * head_dim, head_dim)

    @pl.when(row == 0)
    def spread():
        for head in range(heads):
            q_heads[head] = q_ref[:, columns(head)].astype(jnp.float32)
        for part in range(2):
            new_parts[part] = new_ref[:, columns(part)].astype(jnp.float32)

    queries = jnp.concatenate(
        [q_heads[head, family, :] for head in range(heads)], axis=0
    ).astype(jnp.bfloat16)
    new_keys = new_parts[0, family, :].astype(jnp.bfloat16)
    new_values = new_parts[1, family, :].astype(jnp.bfloat16)
    marks = jnp.concatenate([mask_ref[0]] * heads, axis=0)
    linked = marks[:, :entries]
    held = marks[:, entries : entries + 1]
    step = marks[:, entries + 1 : entries + 2].astype(jnp.int32)
    keys = jnp.concatenate([page[0, :, :head_dim] for page in pages], axis=0)
    values = jnp.concatenate([page[0, :, head_dim:] for page in pages], axis=0)
    first = jnp.maximum(length - WINDOW + 1, 0) // PAGE * PAGE
    shifted = lax.broadcasted_iota(jnp.int32, (1, span), 1) + (first - length + WINDOW)
    contract = (((1,), (1,)), ((), ()))
    scale = head_dim ** (-0.5)
    scores = lax.dot_general(queries, keys, contract, preferred_element_type=jnp.float32) * scale
    scores = jnp.where((shifted < WINDOW) & (shifted > step), scores, NEGATIVE)
    fresh = (
        lax.dot_general(queries, new_keys, contract, preferred_element_type=jnp.float32) * scale
    )
    fresh = jnp.where(linked > 0.5, fresh, NEGATIVE)
    highest = jnp.maximum(
        jnp.max(scores, axis=-1, keepdims=True), jnp.max(fresh, axis=-1, keepdims=True)
    )
    weights = jnp.exp(scores - highest).astype(jnp.bfloat16)
    fresh_weights = jnp.exp(fresh - highest).astype(jnp.bfloat16)
    totals = jnp.sum(weights.astype(jnp.float32), axis=-1, keepdims=True) + jnp.sum(
        fresh_weights.astype(jnp.float32), axis=-1, keepdims=True
    )
    weighted = jnp.dot(weights, values, preferred_element_type=jnp.float32) + jnp.dot(
        fresh_weights, new_values, preferred_element_type=jnp.float32
    )
    answers = jnp.where(held > 0.5, weighted / totals, 0.0)
    for head in range(heads):
        out_heads[head, family, :] = answers[head * entries : (head + 1) * entries]

    @pl.when(row == pl.num_programs(0) - 1)
    def gather_heads():
        for head in range(heads):
            out_ref[:, columns(head)] = out_heads[head].astype(out_ref.dtype)


def attend(local_table, length, pool, queries, entries, marks):
    head_dim = pool.shape[2] // 2
    rows, page_count = local_table.shape
    heads = queries.shape[1] // head_dim

    def page_spec(index):
        return pl.BlockSpec(
            (1, PAGE, 2 * head_dim),
            lambda row, table_ref, length_ref: (table_ref[row * page_count + index], 0, 0),
        )

    def whole(array):
        return pl.BlockSpec(array.shape, lambda row, table_ref, length_ref: (0, 0))

    return pl.pallas_call(
        functools.partial(attention_kernel, page_count, heads, rows),
        out_shape=jax.ShapeDtypeStruct(queries.shape, queries.dtype),
        grid_spec=pltpu.PrefetchScalarGridSpec(
            num_scalar_prefetch=2,
            grid=(rows,),
            in_specs=[page_spec(index) for index in range(page_count)]
            + [
                whole(queries),
                whole(entries),
                pl.BlockSpec(
                    (1,) + marks.shape[1:], lambda row, table_ref, length_ref: (row, 0, 0)
                ),
            ],
            out_specs=whole(queries),
            scratch_shapes=[
                pltpu.VMEM((parts, queries.shape[0], head_dim), jnp.float32)
                for parts in (heads, 2, heads)
            ],
        ),
        compiler_params=pltpu.CompilerParams(vmem_limit_bytes=48 * 2**20),
    )(local_table.reshape(-1), length, *([pool] * page_count), queries, entries, marks)


def on_device(
    x_steps,
    lengths,
    perm,
    parents,
    table,
    pool,
    norm_attn,
    w_query,
    w_keyval,
    w_out,
    norm_mlp,
    w_gate,
    w_up,
    w_down,
):
    steps, rows, width = x_steps.shape
    head_dim = pool.shape[2] // 2
    heads = w_query.shape[1] // head_dim
    req_count = lax.axis_size("req")
    kv_count = lax.axis_size("kv")
    group = lax.axis_index("req")
    member = lax.axis_index("kv")
    halves = kv_count // BEAMS
    half = member // 2 % halves
    beam = member % 2 + 2 * (member // (2 * halves))
    per_group = halves * rows
    group_rows = kv_count * rows
    quota = rows // req_count
    offsets = jnp.arange(rows, dtype=jnp.int32)
    slot_ids = group * per_group + half * rows + offsets
    placed = lax.dynamic_slice_in_dim(perm.reshape(req_count, per_group), half * rows, rows, 1)
    serving = lax.dynamic_index_in_dim(placed, group, 0, keepdims=False)
    target = jnp.sum(
        jnp.where(placed == slot_ids[None, :], jnp.arange(req_count, dtype=jnp.int32)[:, None], 0),
        axis=0,
    )
    anchor = serving // per_group
    to_target = target * quota + rank_within(target, offsets)
    to_anchor = anchor * quota + rank_within(anchor, offsets)
    by_target = to_target[:, None] == offsets[None, :]
    by_anchor = to_anchor[:, None] == offsets[None, :]

    def swap(array):
        shaped = array.reshape(steps, req_count, quota, width)
        return lax.all_to_all(shaped, "req", split_axis=1, concat_axis=1, tiled=True).reshape(
            steps, rows, width
        )

    inputs = reordered(by_anchor, swap(reordered(by_target.T, x_steps)))
    current = inputs.reshape(steps * rows, width)
    length = lengths[serving]
    device = group * kv_count + member

    family = lax.dynamic_slice_in_dim(parents, group * group_rows, group_rows, 1)
    family = family.reshape(steps, kv_count, rows).transpose(1, 0, 2)
    family = pick_half(family, halves, half)
    beams = jnp.arange(BEAMS, dtype=jnp.int32)
    own = jnp.broadcast_to(beams[:, None], (BEAMS, rows))
    origins = [own]
    tables = []
    for step_index in range(steps):
        chosen = family[:, step_index][:, None, :] == beams[None, :, None]
        origins = [jnp.sum(jnp.where(chosen, origin[None], 0), axis=1) for origin in origins]
        origins.append(own)
        tables.append(
            jnp.stack(origins + [jnp.full_like(own, -1)] * (steps - 1 - step_index))
        )
    lineage = jnp.stack(tables)
    held = (lineage[:, 0] == beam).transpose(2, 1, 0)
    linked = lineage[:, 1:, :, :, None] == beams
    linked = linked.transpose(3, 2, 0, 4, 1).reshape(rows, BEAMS * steps, BEAMS * steps)
    step_marks = jnp.broadcast_to(
        jnp.arange(steps, dtype=jnp.int32), (rows, BEAMS, steps)
    )
    marks = jnp.concatenate(
        [
            linked.astype(jnp.float32),
            held.reshape(rows, BEAMS * steps, 1).astype(jnp.float32),
            step_marks.reshape(rows, BEAMS * steps, 1).astype(jnp.float32),
        ],
        axis=2,
    )
    current = gathered(current, kv_count, 1)
    normed = rms_round(pick_half(current, halves, half).reshape(-1, width), norm_attn)
    query = jnp.dot(normed, w_query, preferred_element_type=jnp.float32).astype(jnp.bfloat16)
    fresh = jnp.dot(normed, w_keyval, preferred_element_type=jnp.float32).astype(jnp.bfloat16)
    answers = attend(table - device * pool.shape[0], length, pool, query, fresh, marks)
    answers = answers.reshape(BEAMS, steps * rows, heads * head_dim)
    attended = shared_sum(place_block(answers, halves, half), 2).reshape(-1, heads * head_dim)
    residual = (
        current.reshape(-1, width).astype(jnp.float32)
        + jnp.dot(attended, w_out, preferred_element_type=jnp.float32)
    ).astype(jnp.bfloat16)
    terms = feed_forward(rms_round(residual, norm_mlp), w_gate, w_up, w_down)
    terms = terms.astype(jnp.bfloat16).reshape(kv_count, steps * rows, width)
    summed = reduced(terms, 3)
    residual = lax.dynamic_slice_in_dim(residual, member * steps * rows, steps * rows, 0)
    finished = (residual.astype(jnp.float32) + summed).astype(jnp.bfloat16)
    finished = finished.reshape(steps, rows, width)
    return reordered(by_target, swap(reordered(by_anchor.T, finished)))


def solution(mesh):
    in_specs = (
        P(None, ("req", "kv"), None),
        P(),
        P(),
        P(),
        P(("req", "kv"), None),
        P(("req", "kv"), None, None),
        P(),
        P(),
        P(),
        P(),
        P(),
        P(None, "kv"),
        P(None, "kv"),
        P("kv", None),
    )
    out_specs = P(None, ("req", "kv"), None)
    return jax.shard_map(
        on_device, mesh=mesh, in_specs=in_specs, out_specs=out_specs, check_vma=False
    )
```

```python
import functools

import jax
import jax.numpy as jnp
from jax import lax
from jax.experimental import pallas as pl
from jax.experimental.pallas import tpu as pltpu
from jax.sharding import PartitionSpec as P

WINDOW = 1024
PAGE = 128
BEAMS = 8


EPSILON = 1e-06
NEGATIVE = -1e30


def rms_round(values, gain):
    wide = values.astype(jnp.float32)
    mean_square = jnp.mean(wide * wide, axis=-1, keepdims=True)
    return (wide * lax.rsqrt(mean_square + EPSILON) * gain).astype(jnp.bfloat16)


def feed_forward(mlp_in, w_gate, w_up, w_down):
    gate = jnp.dot(mlp_in, w_gate, preferred_element_type=jnp.float32)
    upward = jnp.dot(mlp_in, w_up, preferred_element_type=jnp.float32)
    hidden = (jax.nn.gelu(gate, approximate=True) * upward).astype(jnp.bfloat16)
    return jnp.dot(hidden, w_down, preferred_element_type=jnp.float32)


def rank_within(labels, offsets):
    earlier = (labels[None, :] == labels[:, None]) & (offsets[None, :] < offsets[:, None])
    return jnp.sum(earlier.astype(jnp.int32), axis=1)


def pick_half(array, halves, half):
    if halves == 1:
        return array
    shaped = array.reshape((BEAMS // 2, halves, 2) + array.shape[1:])
    picked = lax.dynamic_index_in_dim(shaped, half, 1, keepdims=False)
    return picked.reshape((BEAMS,) + array.shape[1:])


def place_block(block, halves, half):
    if halves == 1:
        return block
    whole = jnp.zeros((BEAMS // 2, halves, 2) + block.shape[1:], block.dtype)
    placed = lax.dynamic_update_slice_in_dim(
        whole, block.reshape((BEAMS // 2, 1, 2) + block.shape[1:]), half, 1
    )
    return placed.reshape((BEAMS * halves,) + block.shape[1:])


MESH = pl.DeviceIdType.MESH


class Sends:
    def __init__(self, send_sem):
        self.send_sem = send_sem
        self.started = []

    def go(self, where, source, target, arrived, peer):
        copy = pltpu.make_async_remote_copy(
            src_ref=source,
            dst_ref=target,
            send_sem=self.send_sem.at[len(self.started)],
            recv_sem=arrived,
            device_id={"kv": peer},
            device_id_type=MESH,
        )
        self.started.append((where, copy))
        if where is None:
            copy.start()
        else:
            pl.when(where)(copy.start)

    def finish(self):
        for where, copy in self.started:
            if where is None:
                copy.wait_send()
            else:
                pl.when(where)(copy.wait_send)


def landed(where, target, arrived):
    def wait():
        pltpu.make_async_copy(target, target, arrived).wait()

    if where is None:
        wait()
    else:
        pl.when(where)(wait)


def place_on_lines(count):
    me = lax.axis_index("kv")
    low = lax.rem(me, 2)
    high = me // 2
    length = count // 2
    above, below = high + 1 < length, high > 0
    partner = high * 2 + 1 - low
    up = jnp.minimum(high + 1, length - 1) * 2 + low
    down = jnp.maximum(high - 1, 0) * 2 + low
    return me, low, high, length, above, below, partner, up, down


def greet(above, below, partner, up, down):
    barrier = pltpu.get_barrier_semaphore()

    def hello(peer):
        pl.semaphore_signal(barrier, inc=1, device_id={"kv": peer}, device_id_type=MESH)

    hello(partner)
    pl.when(above)(lambda: hello(up))
    pl.when(below)(lambda: hello(down))
    pl.semaphore_wait(barrier, 1 + above.astype(jnp.int32) + below.astype(jnp.int32))


def column_widths(count, width):
    short = max(width // (count - 2) // 128 * 128, 128)
    return width - short, short


def column_parts(count, width):
    long, short = column_widths(count, width)
    return pl.ds(0, long), pl.ds(long, short)


def gather_kernel(count, greeting, own_ref, all_ref, send_sem, first_sem, second_sem):
    me, low, high, length, above, below, partner, up, down = place_on_lines(count)
    first, second = column_parts(count, own_ref.shape[1])
    if greeting:
        greet(above, below, partner, up, down)
    sends = Sends(send_sem)

    def spread(where, block, source, part, sems, peer):
        sends.go(where, source, all_ref.at[block, :, part], sems.at[block], peer)

    spread(None, me, own_ref.at[:, second], second, second_sem, partner)
    for where, peer in ((above, up), (below, down)):
        spread(where, me, own_ref.at[:, first], first, first_sem, peer)
        spread(where, me, own_ref.at[:, second], second, second_sem, peer)
    spread(None, me, own_ref.at[:, first], first, first_sem, partner)
    all_ref[me] = own_ref[...]
    landed(None, all_ref.at[partner, :, second], second_sem.at[partner])
    for where, peer in ((above, up), (below, down)):
        spread(where, partner, all_ref.at[partner, :, second], second, second_sem, peer)
    for distance in range(1, length):
        for source, here, where, peer in (
            (jnp.maximum(high - distance, 0), high >= distance, above, up),
            (jnp.minimum(high + distance, length - 1), high + distance < length, below, down),
        ):
            same = source * 2 + low
            cross = source * 2 + 1 - low
            onward = here & where
            landed(here, all_ref.at[same, :, first], first_sem.at[same])
            spread(onward, same, all_ref.at[same, :, first], first, first_sem, peer)
            spread(here, same, all_ref.at[same, :, first], first, first_sem, partner)
            landed(here, all_ref.at[same, :, second], second_sem.at[same])
            spread(onward, same, all_ref.at[same, :, second], second, second_sem, peer)
            landed(here, all_ref.at[cross, :, second], second_sem.at[cross])
            spread(onward, cross, all_ref.at[cross, :, second], second, second_sem, peer)
    for line in range(length):
        cross = line * 2 + 1 - low
        landed(None, all_ref.at[cross, :, first], first_sem.at[cross])
    sends.finish()


def gathered(block, count, collective_id):
    whole = pl.BlockSpec(memory_space=pltpu.VMEM)
    return pl.pallas_call(
        functools.partial(gather_kernel, count, True),
        out_shape=jax.ShapeDtypeStruct((count,) + block.shape, block.dtype),
        in_specs=[whole],
        out_specs=whole,
        scratch_shapes=gather_semaphores(count),
        compiler_params=pltpu.CompilerParams(
            collective_id=collective_id, has_side_effects=True, vmem_limit_bytes=40 * 2**20
        ),
    )(block)


def reduce_kernel(
    count,
    terms_ref,
    sum_ref,
    cross_first,
    up_first,
    down_first,
    stage_first,
    cross_second,
    up_second,
    down_second,
    stage_second,
    stage_cross,
    send_sem,
    cross_sem,
    up_sem,
    down_sem,
):
    me, low, high, length, above, below, partner, up, down = place_on_lines(count)
    first, second = column_parts(count, sum_ref.shape[1])
    greet(above, below, partner, up, down)
    sends = Sends(send_sem)
    for line in range(length):
        sends.go(
            None,
            terms_ref.at[line * 2 + 1 - low, :, first],
            cross_first.at[line],
            cross_sem.at[line],
            partner,
        )

    def wide(ref):
        return ref[...].astype(jnp.float32)

    def base_first(line):
        return wide(terms_ref.at[line * 2 + low, :, first]) + wide(cross_first.at[line])

    def pass_on(here, line, behind, slot, stage, arrived, ahead, base):
        def with_slot():
            stage[...] = (base() + wide(slot)).astype(stage.dtype)

        def alone():
            stage[...] = base().astype(stage.dtype)

        landed(here & behind, slot, arrived)
        pl.when(here & behind)(with_slot)
        pl.when(here & jnp.logical_not(behind))(alone)
        sends.go(here, stage, slot, arrived, ahead)

    directions = (
        (1, below, up_second, up_first, up_sem, up),
        (-1, above, down_second, down_first, down_sem, down),
    )
    for distance in range(length - 1, 0, -1):
        for sign, behind, slot, _, sems, ahead in directions:
            line = high + sign * distance
            here = (line < length) & (line >= 0)
            line = jnp.clip(line, 0, length - 1)
            for other in range(2):
                side = low if other == 0 else 1 - low
                block = line * 2 + side
                pass_on(
                    here,
                    line,
                    behind,
                    slot.at[block],
                    stage_second.at[block],
                    sems.at[length + block],
                    ahead,
                    lambda block=block: wide(terms_ref.at[block, :, second]),
                )
    for line in range(length):
        landed(None, cross_first.at[line], cross_sem.at[line])
    for distance in range(length - 1, 0, -1):
        for sign, behind, _, slot, sems, ahead in directions:
            line = high + sign * distance
            here = (line < length) & (line >= 0)
            line = jnp.clip(line, 0, length - 1)
            pass_on(
                here,
                line,
                behind,
                slot.at[line],
                stage_first.at[line],
                sems.at[line],
                ahead,
                lambda line=line: base_first(line),
            )

    def collect(into, part, value, up_slot, down_slot, up_arrived, down_arrived):
        into[:, part] = value
        landed(below, up_slot, up_arrived)
        landed(above, down_slot, down_arrived)

        def add(slot):
            into[:, part] += wide(slot)

        pl.when(below)(lambda: add(up_slot))
        pl.when(above)(lambda: add(down_slot))

    collect(
        sum_ref,
        second,
        wide(terms_ref.at[partner, :, second]),
        up_second.at[partner],
        down_second.at[partner],
        up_sem.at[length + partner],
        down_sem.at[length + partner],
    )
    stage_cross[...] = sum_ref[:, second].astype(stage_cross.dtype)
    sends.go(None, stage_cross, cross_second, cross_sem.at[length], partner)
    collect(
        sum_ref,
        second,
        wide(terms_ref.at[me, :, second]),
        up_second.at[me],
        down_second.at[me],
        up_sem.at[length + me],
        down_sem.at[length + me],
    )
    collect(
        sum_ref,
        first,
        base_first(high),
        up_first.at[high],
        down_first.at[high],
        up_sem.at[high],
        down_sem.at[high],
    )
    landed(None, cross_second, cross_sem.at[length])
    sum_ref[:, second] += wide(cross_second)
    sends.finish()


def gather_semaphores(count):
    return [
        pltpu.SemaphoreType.DMA((8 + 10 * (count // 2),)),
        pltpu.SemaphoreType.DMA((count,)),
        pltpu.SemaphoreType.DMA((count,)),
    ]


def reduce_scratch(terms):
    count, rows, width = terms.shape
    length = count // 2

    long, short = column_widths(count, width)

    def slots(columns, *shape):
        return pltpu.VMEM(shape + (rows, columns), terms.dtype)

    return [
        slots(long, length),
        slots(long, length),
        slots(long, length),
        slots(long, length),
        slots(short),
        slots(short, count),
        slots(short, count),
        slots(short, count),
        slots(short),
        pltpu.SemaphoreType.DMA((8 * length,)),
        pltpu.SemaphoreType.DMA((length + 1,)),
        pltpu.SemaphoreType.DMA((length + count,)),
        pltpu.SemaphoreType.DMA((length + count,)),
    ]


def reduced(terms, collective_id):
    count, rows, width = terms.shape
    whole = pl.BlockSpec(memory_space=pltpu.VMEM)
    return pl.pallas_call(
        functools.partial(reduce_kernel, count),
        out_shape=jax.ShapeDtypeStruct((rows, width), jnp.float32),
        in_specs=[whole],
        out_specs=whole,
        scratch_shapes=reduce_scratch(terms),
        compiler_params=pltpu.CompilerParams(
            collective_id=collective_id, has_side_effects=True, vmem_limit_bytes=40 * 2**20
        ),
    )(terms)


def share_kernel(count, terms_ref, all_ref, sum_ref, own_ref, *scratch):
    reduce_kernel(count, terms_ref, sum_ref, *scratch[:-3])
    own_ref[...] = sum_ref[...].astype(own_ref.dtype)
    gather_kernel(count, False, own_ref, all_ref, *scratch[-3:])


def shared_sum(terms, collective_id):
    count, rows, width = terms.shape
    whole = pl.BlockSpec(memory_space=pltpu.VMEM)
    return pl.pallas_call(
        functools.partial(share_kernel, count),
        out_shape=jax.ShapeDtypeStruct(terms.shape, terms.dtype),
        in_specs=[whole],
        out_specs=whole,
        scratch_shapes=[
            pltpu.VMEM((rows, width), jnp.float32),
            pltpu.VMEM((rows, width), terms.dtype),
        ]
        + reduce_scratch(terms)
        + gather_semaphores(count),
        compiler_params=pltpu.CompilerParams(
            collective_id=collective_id, has_side_effects=True, vmem_limit_bytes=40 * 2**20
        ),
    )(terms)


def reordered(selector, array):
    return jnp.einsum(
        "pi,tiw->tpw", selector.astype(jnp.bfloat16), array, preferred_element_type=jnp.float32
    ).astype(jnp.bfloat16)


def attention_kernel(page_count, heads, stride, table_ref, length_ref, *refs):
    pages = refs[:page_count]
    q_ref, new_ref, mask_ref, out_ref, q_heads, new_parts, out_heads = refs[page_count:]
    row = pl.program_id(0)
    length = length_ref[row]
    entries = mask_ref.shape[1]
    head_dim = q_ref.shape[1] // heads
    span = page_count * PAGE
    family = pl.ds(row, entries, stride=stride)

    def columns(part):
        return pl.ds(part * head_dim, head_dim)

    @pl.when(row == 0)
    def spread():
        for head in range(heads):
            q_heads[head] = q_ref[:, columns(head)].astype(jnp.float32)
        for part in range(2):
            new_parts[part] = new_ref[:, columns(part)].astype(jnp.float32)

    queries = jnp.concatenate(
        [q_heads[head, family, :] for head in range(heads)], axis=0
    ).astype(jnp.bfloat16)
    new_keys = new_parts[0, family, :].astype(jnp.bfloat16)
    new_values = new_parts[1, family, :].astype(jnp.bfloat16)
    marks = jnp.concatenate([mask_ref[0]] * heads, axis=0)
    linked = marks[:, :entries]
    held = marks[:, entries : entries + 1]
    step = marks[:, entries + 1 : entries + 2].astype(jnp.int32)
    keys = jnp.concatenate([page[0, :, :head_dim] for page in pages], axis=0)
    values = jnp.concatenate([page[0, :, head_dim:] for page in pages], axis=0)
    first = jnp.maximum(length - WINDOW + 1, 0) // PAGE * PAGE
    shifted = lax.broadcasted_iota(jnp.int32, (1, span), 1) + (first - length + WINDOW)
    contract = (((1,), (1,)), ((), ()))
    scale = head_dim ** (-0.5)
    scores = lax.dot_general(queries, keys, contract, preferred_element_type=jnp.float32) * scale
    scores = jnp.where((shifted < WINDOW) & (shifted > step), scores, NEGATIVE)
    fresh = (
        lax.dot_general(queries, new_keys, contract, preferred_element_type=jnp.float32) * scale
    )
    fresh = jnp.where(linked > 0.5, fresh, NEGATIVE)
    highest = jnp.maximum(
        jnp.max(scores, axis=-1, keepdims=True), jnp.max(fresh, axis=-1, keepdims=True)
    )
    weights = jnp.exp(scores - highest).astype(jnp.bfloat16)
    fresh_weights = jnp.exp(fresh - highest).astype(jnp.bfloat16)
    totals = jnp.sum(weights.astype(jnp.float32), axis=-1, keepdims=True) + jnp.sum(
        fresh_weights.astype(jnp.float32), axis=-1, keepdims=True
    )
    weighted = jnp.dot(weights, values, preferred_element_type=jnp.float32) + jnp.dot(
        fresh_weights, new_values, preferred_element_type=jnp.float32
    )
    answers = jnp.where(held > 0.5, weighted / totals, 0.0)
    for head in range(heads):
        out_heads[head, family, :] = answers[head * entries : (head + 1) * entries]

    @pl.when(row == pl.num_programs(0) - 1)
    def gather_heads():
        for head in range(heads):
            out_ref[:, columns(head)] = out_heads[head].astype(out_ref.dtype)


def attend(local_table, length, pool, queries, entries, marks):
    head_dim = pool.shape[2] // 2
    rows, page_count = local_table.shape
    heads = queries.shape[1] // head_dim

    def page_spec(index):
        return pl.BlockSpec(
            (1, PAGE, 2 * head_dim),
            lambda row, table_ref, length_ref: (table_ref[row * page_count + index], 0, 0),
        )

    def whole(array):
        return pl.BlockSpec(array.shape, lambda row, table_ref, length_ref: (0, 0))

    return pl.pallas_call(
        functools.partial(attention_kernel, page_count, heads, rows),
        out_shape=jax.ShapeDtypeStruct(queries.shape, queries.dtype),
        grid_spec=pltpu.PrefetchScalarGridSpec(
            num_scalar_prefetch=2,
            grid=(rows,),
            in_specs=[page_spec(index) for index in range(page_count)]
            + [
                whole(queries),
                whole(entries),
                pl.BlockSpec(
                    (1,) + marks.shape[1:], lambda row, table_ref, length_ref: (row, 0, 0)
                ),
            ],
            out_specs=whole(queries),
            scratch_shapes=[
                pltpu.VMEM((parts, queries.shape[0], head_dim), jnp.float32)
                for parts in (heads, 2, heads)
            ],
        ),
        compiler_params=pltpu.CompilerParams(vmem_limit_bytes=48 * 2**20),
    )(local_table.reshape(-1), length, *([pool] * page_count), queries, entries, marks)


def on_device(
    x_steps,
    lengths,
    perm,
    parents,
    table,
    pool,
    norm_attn,
    w_query,
    w_keyval,
    w_out,
    norm_mlp,
    w_gate,
    w_up,
    w_down,
):
    steps, rows, width = x_steps.shape
    head_dim = pool.shape[2] // 2
    heads = w_query.shape[1] // head_dim
    req_count = lax.axis_size("req")
    kv_count = lax.axis_size("kv")
    group = lax.axis_index("req")
    member = lax.axis_index("kv")
    halves = kv_count // BEAMS
    half = member // 2 % halves
    beam = member % 2 + 2 * (member // (2 * halves))
    per_group = halves * rows
    group_rows = kv_count * rows
    quota = rows // req_count
    offsets = jnp.arange(rows, dtype=jnp.int32)
    slot_ids = group * per_group + half * rows + offsets
    placed = lax.dynamic_slice_in_dim(perm.reshape(req_count, per_group), half * rows, rows, 1)
    serving = lax.dynamic_index_in_dim(placed, group, 0, keepdims=False)
    target = jnp.sum(
        jnp.where(placed == slot_ids[None, :], jnp.arange(req_count, dtype=jnp.int32)[:, None], 0),
        axis=0,
    )
    anchor = serving // per_group
    to_target = target * quota + rank_within(target, offsets)
    to_anchor = anchor * quota + rank_within(anchor, offsets)
    by_target = to_target[:, None] == offsets[None, :]
    by_anchor = to_anchor[:, None] == offsets[None, :]

    def swap(array):
        shaped = array.reshape(steps, req_count, quota, width)
        return lax.all_to_all(shaped, "req", split_axis=1, concat_axis=1, tiled=True).reshape(
            steps, rows, width
        )

    inputs = reordered(by_anchor, swap(reordered(by_target.T, x_steps)))
    current = inputs.reshape(steps * rows, width)
    length = lengths[serving]
    device = group * kv_count + member

    family = lax.dynamic_slice_in_dim(parents, group * group_rows, group_rows, 1)
    family = family.reshape(steps, kv_count, rows).transpose(1, 0, 2)
    family = pick_half(family, halves, half)
    beams = jnp.arange(BEAMS, dtype=jnp.int32)
    own = jnp.broadcast_to(beams[:, None], (BEAMS, rows))
    origins = [own]
    tables = []
    for step_index in range(steps):
        chosen = family[:, step_index][:, None, :] == beams[None, :, None]
        origins = [jnp.sum(jnp.where(chosen, origin[None], 0), axis=1) for origin in origins]
        origins.append(own)
        tables.append(
            jnp.stack(origins + [jnp.full_like(own, -1)] * (steps - 1 - step_index))
        )
    lineage = jnp.stack(tables)
    held = (lineage[:, 0] == beam).transpose(2, 1, 0)
    linked = lineage[:, 1:, :, :, None] == beams
    linked = linked.transpose(3, 2, 0, 4, 1).reshape(rows, BEAMS * steps, BEAMS * steps)
    step_marks = jnp.broadcast_to(
        jnp.arange(steps, dtype=jnp.int32), (rows, BEAMS, steps)
    )
    marks = jnp.concatenate(
        [
            linked.astype(jnp.float32),
            held.reshape(rows, BEAMS * steps, 1).astype(jnp.float32),
            step_marks.reshape(rows, BEAMS * steps, 1).astype(jnp.float32),
        ],
        axis=2,
    )
    current = gathered(current, kv_count, 1)
    normed = rms_round(pick_half(current, halves, half).reshape(-1, width), norm_attn)
    query = jnp.dot(normed, w_query, preferred_element_type=jnp.float32).astype(jnp.bfloat16)
    fresh = jnp.dot(normed, w_keyval, preferred_element_type=jnp.float32).astype(jnp.bfloat16)
    answers = attend(table - device * pool.shape[0], length, pool, query, fresh, marks)
    answers = answers.reshape(BEAMS, steps * rows, heads * head_dim)
    attended = shared_sum(place_block(answers, halves, half), 2).reshape(-1, heads * head_dim)
    residual = (
        current.reshape(-1, width).astype(jnp.float32)
        + jnp.dot(attended, w_out, preferred_element_type=jnp.float32)
    ).astype(jnp.bfloat16)
    terms = feed_forward(rms_round(residual, norm_mlp), w_gate, w_up, w_down)
    terms = terms.astype(jnp.bfloat16).reshape(kv_count, steps * rows, width)
    summed = reduced(terms, 3)
    residual = lax.dynamic_slice_in_dim(residual, member * steps * rows, steps * rows, 0)
    finished = (residual.astype(jnp.float32) + summed).astype(jnp.bfloat16)
    finished = finished.reshape(steps, rows, width)
    return reordered(by_target, swap(reordered(by_anchor.T, finished)))


def solution(mesh):
    in_specs = (
        P(None, ("req", "kv"), None),
        P(),
        P(),
        P(),
        P(("req", "kv"), None),
        P(("req", "kv"), None, None),
        P(),
        P(),
        P(),
        P(),
        P(),
        P(None, "kv"),
        P(None, "kv"),
        P("kv", None),
    )
    out_specs = P(None, ("req", "kv"), None)
    return jax.shard_map(
        on_device, mesh=mesh, in_specs=in_specs, out_specs=out_specs, check_vma=False
    )
```

```python
import functools

import jax
import jax.numpy as jnp
from jax import lax
from jax.experimental import pallas as pl
from jax.experimental.pallas import tpu as pltpu
from jax.sharding import PartitionSpec as P

WINDOW = 1024
PAGE = 128
BEAMS = 8


EPSILON = 1e-06
NEGATIVE = -1e30


def rms_round(values, gain):
    wide = values.astype(jnp.float32)
    mean_square = jnp.mean(wide * wide, axis=-1, keepdims=True)
    return (wide * lax.rsqrt(mean_square + EPSILON) * gain).astype(jnp.bfloat16)


def feed_forward(mlp_in, w_gate, w_up, w_down):
    gate = jnp.dot(mlp_in, w_gate, preferred_element_type=jnp.float32)
    upward = jnp.dot(mlp_in, w_up, preferred_element_type=jnp.float32)
    hidden = (jax.nn.gelu(gate, approximate=True) * upward).astype(jnp.bfloat16)
    return jnp.dot(hidden, w_down, preferred_element_type=jnp.float32)


def rank_within(labels, offsets):
    earlier = (labels[None, :] == labels[:, None]) & (offsets[None, :] < offsets[:, None])
    return jnp.sum(earlier.astype(jnp.int32), axis=1)


def pick_half(array, halves, half):
    if halves == 1:
        return array
    shaped = array.reshape((BEAMS // 2, halves, 2) + array.shape[1:])
    picked = lax.dynamic_index_in_dim(shaped, half, 1, keepdims=False)
    return picked.reshape((BEAMS,) + array.shape[1:])


def place_block(block, halves, half):
    if halves == 1:
        return block
    whole = jnp.zeros((BEAMS // 2, halves, 2) + block.shape[1:], block.dtype)
    placed = lax.dynamic_update_slice_in_dim(
        whole, block.reshape((BEAMS // 2, 1, 2) + block.shape[1:]), half, 1
    )
    return placed.reshape((BEAMS * halves,) + block.shape[1:])


MESH = pl.DeviceIdType.MESH


class Sends:
    def __init__(self, send_sem):
        self.send_sem = send_sem
        self.started = []

    def go(self, where, source, target, arrived, peer):
        copy = pltpu.make_async_remote_copy(
            src_ref=source,
            dst_ref=target,
            send_sem=self.send_sem.at[len(self.started)],
            recv_sem=arrived,
            device_id={"kv": peer},
            device_id_type=MESH,
        )
        self.started.append((where, copy))
        if where is None:
            copy.start()
        else:
            pl.when(where)(copy.start)

    def finish(self):
        for where, copy in self.started:
            if where is None:
                copy.wait_send()
            else:
                pl.when(where)(copy.wait_send)


def landed(where, target, arrived):
    def wait():
        pltpu.make_async_copy(target, target, arrived).wait()

    if where is None:
        wait()
    else:
        pl.when(where)(wait)


def place_on_lines(count):
    me = lax.axis_index("kv")
    low = lax.rem(me, 2)
    high = me // 2
    length = count // 2
    above, below = high + 1 < length, high > 0
    partner = high * 2 + 1 - low
    up = jnp.minimum(high + 1, length - 1) * 2 + low
    down = jnp.maximum(high - 1, 0) * 2 + low
    return me, low, high, length, above, below, partner, up, down


def greet(above, below, partner, up, down):
    barrier = pltpu.get_barrier_semaphore()

    def hello(peer):
        pl.semaphore_signal(barrier, inc=1, device_id={"kv": peer}, device_id_type=MESH)

    hello(partner)
    pl.when(above)(lambda: hello(up))
    pl.when(below)(lambda: hello(down))
    pl.semaphore_wait(barrier, 1 + above.astype(jnp.int32) + below.astype(jnp.int32))


def gather_kernel(count, greeting, own_ref, all_ref, send_sem, first_sem, second_sem):
    me, low, high, length, above, below, partner, up, down = place_on_lines(count)
    middle = own_ref.shape[0] // 2
    first, second = pl.ds(0, middle), pl.ds(middle, middle)
    if greeting:
        greet(above, below, partner, up, down)
    sends = Sends(send_sem)

    def spread(where, block, source, part, sems, peer):
        sends.go(where, source, all_ref.at[block, part], sems.at[block], peer)

    spread(None, me, own_ref.at[second], second, second_sem, partner)
    for where, peer in ((above, up), (below, down)):
        spread(where, me, own_ref.at[first], first, first_sem, peer)
        spread(where, me, own_ref.at[second], second, second_sem, peer)
    spread(None, me, own_ref.at[first], first, first_sem, partner)
    all_ref[me] = own_ref[...]
    landed(None, all_ref.at[partner, second], second_sem.at[partner])
    for where, peer in ((above, up), (below, down)):
        spread(where, partner, all_ref.at[partner, second], second, second_sem, peer)
    for distance in range(1, length):
        for source, here, where, peer in (
            (jnp.maximum(high - distance, 0), high >= distance, above, up),
            (jnp.minimum(high + distance, length - 1), high + distance < length, below, down),
        ):
            same = source * 2 + low
            cross = source * 2 + 1 - low
            onward = here & where
            landed(here, all_ref.at[same, first], first_sem.at[same])
            spread(onward, same, all_ref.at[same, first], first, first_sem, peer)
            spread(here, same, all_ref.at[same, first], first, first_sem, partner)
            landed(here, all_ref.at[same, second], second_sem.at[same])
            spread(onward, same, all_ref.at[same, second], second, second_sem, peer)
            landed(here, all_ref.at[cross, second], second_sem.at[cross])
            spread(onward, cross, all_ref.at[cross, second], second, second_sem, peer)
    for line in range(length):
        cross = line * 2 + 1 - low
        landed(None, all_ref.at[cross, first], first_sem.at[cross])
    sends.finish()


def gathered(block, count, collective_id):
    whole = pl.BlockSpec(memory_space=pltpu.VMEM)
    return pl.pallas_call(
        functools.partial(gather_kernel, count, True),
        out_shape=jax.ShapeDtypeStruct((count,) + block.shape, block.dtype),
        in_specs=[whole],
        out_specs=whole,
        scratch_shapes=gather_semaphores(count),
        compiler_params=pltpu.CompilerParams(
            collective_id=collective_id, has_side_effects=True, vmem_limit_bytes=40 * 2**20
        ),
    )(block)


def reduce_kernel(
    count,
    terms_ref,
    sum_ref,
    cross_first,
    up_first,
    down_first,
    stage_first,
    cross_second,
    up_second,
    down_second,
    stage_second,
    stage_cross,
    send_sem,
    cross_sem,
    up_sem,
    down_sem,
):
    me, low, high, length, above, below, partner, up, down = place_on_lines(count)
    middle = sum_ref.shape[0] // 2
    first, second = pl.ds(0, middle), pl.ds(middle, middle)
    greet(above, below, partner, up, down)
    sends = Sends(send_sem)
    for line in range(length):
        sends.go(
            None,
            terms_ref.at[line * 2 + 1 - low, first],
            cross_first.at[line],
            cross_sem.at[line],
            partner,
        )

    def wide(ref):
        return ref[...].astype(jnp.float32)

    def base_first(line):
        return wide(terms_ref.at[line * 2 + low, first]) + wide(cross_first.at[line])

    def pass_on(here, line, behind, slot, stage, arrived, ahead, base):
        def with_slot():
            stage[...] = (base() + wide(slot)).astype(stage.dtype)

        def alone():
            stage[...] = base().astype(stage.dtype)

        landed(here & behind, slot, arrived)
        pl.when(here & behind)(with_slot)
        pl.when(here & jnp.logical_not(behind))(alone)
        sends.go(here, stage, slot, arrived, ahead)

    directions = (
        (1, below, up_second, up_first, up_sem, up),
        (-1, above, down_second, down_first, down_sem, down),
    )
    for distance in range(length - 1, 0, -1):
        for sign, behind, slot, _, sems, ahead in directions:
            line = high + sign * distance
            here = (line < length) & (line >= 0)
            line = jnp.clip(line, 0, length - 1)
            for other in range(2):
                side = low if other == 0 else 1 - low
                block = line * 2 + side
                pass_on(
                    here,
                    line,
                    behind,
                    slot.at[block],
                    stage_second.at[block],
                    sems.at[length + block],
                    ahead,
                    lambda block=block: wide(terms_ref.at[block, second]),
                )
        for sign, behind, _, slot, sems, ahead in directions:
            line = high + sign * distance
            here = (line < length) & (line >= 0)
            line = jnp.clip(line, 0, length - 1)
            landed(here, cross_first.at[line], cross_sem.at[line])
            pass_on(
                here,
                line,
                behind,
                slot.at[line],
                stage_first.at[line],
                sems.at[line],
                ahead,
                lambda line=line: base_first(line),
            )
    landed(None, cross_first.at[high], cross_sem.at[high])

    def collect(into, part, value, up_slot, down_slot, up_arrived, down_arrived):
        into[part, :] = value
        landed(below, up_slot, up_arrived)
        landed(above, down_slot, down_arrived)

        def add(slot):
            into[part, :] += wide(slot)

        pl.when(below)(lambda: add(up_slot))
        pl.when(above)(lambda: add(down_slot))

    collect(
        sum_ref,
        second,
        wide(terms_ref.at[partner, second]),
        up_second.at[partner],
        down_second.at[partner],
        up_sem.at[length + partner],
        down_sem.at[length + partner],
    )
    stage_cross[...] = sum_ref[second, :].astype(stage_cross.dtype)
    sends.go(None, stage_cross, cross_second, cross_sem.at[length], partner)
    collect(
        sum_ref,
        second,
        wide(terms_ref.at[me, second]),
        up_second.at[me],
        down_second.at[me],
        up_sem.at[length + me],
        down_sem.at[length + me],
    )
    collect(
        sum_ref,
        first,
        base_first(high),
        up_first.at[high],
        down_first.at[high],
        up_sem.at[high],
        down_sem.at[high],
    )
    landed(None, cross_second, cross_sem.at[length])
    sum_ref[second, :] += wide(cross_second)
    sends.finish()


def gather_semaphores(count):
    return [
        pltpu.SemaphoreType.DMA((8 + 10 * (count // 2),)),
        pltpu.SemaphoreType.DMA((count,)),
        pltpu.SemaphoreType.DMA((count,)),
    ]


def reduce_scratch(terms):
    count, rows, width = terms.shape
    length = count // 2

    def slots(*shape):
        return pltpu.VMEM(shape + (rows // 2, width), terms.dtype)

    return [
        slots(length),
        slots(length),
        slots(length),
        slots(length),
        slots(),
        slots(count),
        slots(count),
        slots(count),
        slots(),
        pltpu.SemaphoreType.DMA((8 * length,)),
        pltpu.SemaphoreType.DMA((length + 1,)),
        pltpu.SemaphoreType.DMA((length + count,)),
        pltpu.SemaphoreType.DMA((length + count,)),
    ]


def reduced(terms, collective_id):
    count, rows, width = terms.shape
    whole = pl.BlockSpec(memory_space=pltpu.VMEM)
    return pl.pallas_call(
        functools.partial(reduce_kernel, count),
        out_shape=jax.ShapeDtypeStruct((rows, width), jnp.float32),
        in_specs=[whole],
        out_specs=whole,
        scratch_shapes=reduce_scratch(terms),
        compiler_params=pltpu.CompilerParams(
            collective_id=collective_id, has_side_effects=True, vmem_limit_bytes=40 * 2**20
        ),
    )(terms)


def share_kernel(count, terms_ref, all_ref, sum_ref, own_ref, *scratch):
    reduce_kernel(count, terms_ref, sum_ref, *scratch[:-3])
    own_ref[...] = sum_ref[...].astype(own_ref.dtype)
    gather_kernel(count, False, own_ref, all_ref, *scratch[-3:])


def shared_sum(terms, collective_id):
    count, rows, width = terms.shape
    whole = pl.BlockSpec(memory_space=pltpu.VMEM)
    return pl.pallas_call(
        functools.partial(share_kernel, count),
        out_shape=jax.ShapeDtypeStruct(terms.shape, terms.dtype),
        in_specs=[whole],
        out_specs=whole,
        scratch_shapes=[
            pltpu.VMEM((rows, width), jnp.float32),
            pltpu.VMEM((rows, width), terms.dtype),
        ]
        + reduce_scratch(terms)
        + gather_semaphores(count),
        compiler_params=pltpu.CompilerParams(
            collective_id=collective_id, has_side_effects=True, vmem_limit_bytes=40 * 2**20
        ),
    )(terms)


def reordered(selector, array):
    return jnp.einsum(
        "pi,tiw->tpw", selector.astype(jnp.bfloat16), array, preferred_element_type=jnp.float32
    ).astype(jnp.bfloat16)


def attention_kernel(page_count, heads, stride, table_ref, length_ref, *refs):
    pages = refs[:page_count]
    q_ref, new_ref, mask_ref, out_ref, q_heads, new_parts, out_heads = refs[page_count:]
    row = pl.program_id(0)
    length = length_ref[row]
    entries = mask_ref.shape[1]
    head_dim = q_ref.shape[1] // heads
    span = page_count * PAGE
    family = pl.ds(row, entries, stride=stride)

    def columns(part):
        return pl.ds(part * head_dim, head_dim)

    @pl.when(row == 0)
    def spread():
        for head in range(heads):
            q_heads[head] = q_ref[:, columns(head)].astype(jnp.float32)
        for part in range(2):
            new_parts[part] = new_ref[:, columns(part)].astype(jnp.float32)

    queries = jnp.concatenate(
        [q_heads[head, family, :] for head in range(heads)], axis=0
    ).astype(jnp.bfloat16)
    new_keys = new_parts[0, family, :].astype(jnp.bfloat16)
    new_values = new_parts[1, family, :].astype(jnp.bfloat16)
    marks = jnp.concatenate([mask_ref[0]] * heads, axis=0)
    linked = marks[:, :entries]
    held = marks[:, entries : entries + 1]
    step = marks[:, entries + 1 : entries + 2].astype(jnp.int32)
    keys = jnp.concatenate([page[0, :, :head_dim] for page in pages], axis=0)
    values = jnp.concatenate([page[0, :, head_dim:] for page in pages], axis=0)
    first = jnp.maximum(length - WINDOW + 1, 0) // PAGE * PAGE
    shifted = lax.broadcasted_iota(jnp.int32, (1, span), 1) + (first - length + WINDOW)
    contract = (((1,), (1,)), ((), ()))
    scale = head_dim ** (-0.5)
    scores = lax.dot_general(queries, keys, contract, preferred_element_type=jnp.float32) * scale
    scores = jnp.where((shifted < WINDOW) & (shifted > step), scores, NEGATIVE)
    fresh = (
        lax.dot_general(queries, new_keys, contract, preferred_element_type=jnp.float32) * scale
    )
    fresh = jnp.where(linked > 0.5, fresh, NEGATIVE)
    highest = jnp.maximum(
        jnp.max(scores, axis=-1, keepdims=True), jnp.max(fresh, axis=-1, keepdims=True)
    )
    weights = jnp.exp(scores - highest).astype(jnp.bfloat16)
    fresh_weights = jnp.exp(fresh - highest).astype(jnp.bfloat16)
    totals = jnp.sum(weights.astype(jnp.float32), axis=-1, keepdims=True) + jnp.sum(
        fresh_weights.astype(jnp.float32), axis=-1, keepdims=True
    )
    weighted = jnp.dot(weights, values, preferred_element_type=jnp.float32) + jnp.dot(
        fresh_weights, new_values, preferred_element_type=jnp.float32
    )
    answers = jnp.where(held > 0.5, weighted / totals, 0.0)
    for head in range(heads):
        out_heads[head, family, :] = answers[head * entries : (head + 1) * entries]

    @pl.when(row == pl.num_programs(0) - 1)
    def gather_heads():
        for head in range(heads):
            out_ref[:, columns(head)] = out_heads[head].astype(out_ref.dtype)


def attend(local_table, length, pool, queries, entries, marks):
    head_dim = pool.shape[2] // 2
    rows, page_count = local_table.shape
    heads = queries.shape[1] // head_dim

    def page_spec(index):
        return pl.BlockSpec(
            (1, PAGE, 2 * head_dim),
            lambda row, table_ref, length_ref: (table_ref[row * page_count + index], 0, 0),
        )

    def whole(array):
        return pl.BlockSpec(array.shape, lambda row, table_ref, length_ref: (0, 0))

    return pl.pallas_call(
        functools.partial(attention_kernel, page_count, heads, rows),
        out_shape=jax.ShapeDtypeStruct(queries.shape, queries.dtype),
        grid_spec=pltpu.PrefetchScalarGridSpec(
            num_scalar_prefetch=2,
            grid=(rows,),
            in_specs=[page_spec(index) for index in range(page_count)]
            + [
                whole(queries),
                whole(entries),
                pl.BlockSpec(
                    (1,) + marks.shape[1:], lambda row, table_ref, length_ref: (row, 0, 0)
                ),
            ],
            out_specs=whole(queries),
            scratch_shapes=[
                pltpu.VMEM((parts, queries.shape[0], head_dim), jnp.float32)
                for parts in (heads, 2, heads)
            ],
        ),
        compiler_params=pltpu.CompilerParams(vmem_limit_bytes=48 * 2**20),
    )(local_table.reshape(-1), length, *([pool] * page_count), queries, entries, marks)


def on_device(
    x_steps,
    lengths,
    perm,
    parents,
    table,
    pool,
    norm_attn,
    w_query,
    w_keyval,
    w_out,
    norm_mlp,
    w_gate,
    w_up,
    w_down,
):
    steps, rows, width = x_steps.shape
    head_dim = pool.shape[2] // 2
    heads = w_query.shape[1] // head_dim
    req_count = lax.axis_size("req")
    kv_count = lax.axis_size("kv")
    group = lax.axis_index("req")
    member = lax.axis_index("kv")
    halves = kv_count // BEAMS
    half = member // 2 % halves
    beam = member % 2 + 2 * (member // (2 * halves))
    per_group = halves * rows
    group_rows = kv_count * rows
    quota = rows // req_count
    offsets = jnp.arange(rows, dtype=jnp.int32)
    slot_ids = group * per_group + half * rows + offsets
    placed = lax.dynamic_slice_in_dim(perm.reshape(req_count, per_group), half * rows, rows, 1)
    serving = lax.dynamic_index_in_dim(placed, group, 0, keepdims=False)
    target = jnp.sum(
        jnp.where(placed == slot_ids[None, :], jnp.arange(req_count, dtype=jnp.int32)[:, None], 0),
        axis=0,
    )
    anchor = serving // per_group
    to_target = target * quota + rank_within(target, offsets)
    to_anchor = anchor * quota + rank_within(anchor, offsets)
    by_target = to_target[:, None] == offsets[None, :]
    by_anchor = to_anchor[:, None] == offsets[None, :]

    def swap(array):
        shaped = array.reshape(steps, req_count, quota, width)
        return lax.all_to_all(shaped, "req", split_axis=1, concat_axis=1, tiled=True).reshape(
            steps, rows, width
        )

    inputs = reordered(by_anchor, swap(reordered(by_target.T, x_steps)))
    current = inputs.reshape(steps * rows, width)
    length = lengths[serving]
    device = group * kv_count + member

    family = lax.dynamic_slice_in_dim(parents, group * group_rows, group_rows, 1)
    family = family.reshape(steps, kv_count, rows).transpose(1, 0, 2)
    family = pick_half(family, halves, half)
    beams = jnp.arange(BEAMS, dtype=jnp.int32)
    own = jnp.broadcast_to(beams[:, None], (BEAMS, rows))
    origins = [own]
    tables = []
    for step_index in range(steps):
        chosen = family[:, step_index][:, None, :] == beams[None, :, None]
        origins = [jnp.sum(jnp.where(chosen, origin[None], 0), axis=1) for origin in origins]
        origins.append(own)
        tables.append(
            jnp.stack(origins + [jnp.full_like(own, -1)] * (steps - 1 - step_index))
        )
    lineage = jnp.stack(tables)
    held = (lineage[:, 0] == beam).transpose(2, 1, 0)
    linked = lineage[:, 1:, :, :, None] == beams
    linked = linked.transpose(3, 2, 0, 4, 1).reshape(rows, BEAMS * steps, BEAMS * steps)
    step_marks = jnp.broadcast_to(
        jnp.arange(steps, dtype=jnp.int32), (rows, BEAMS, steps)
    )
    marks = jnp.concatenate(
        [
            linked.astype(jnp.float32),
            held.reshape(rows, BEAMS * steps, 1).astype(jnp.float32),
            step_marks.reshape(rows, BEAMS * steps, 1).astype(jnp.float32),
        ],
        axis=2,
    )
    current = gathered(current, kv_count, 1)
    normed = rms_round(pick_half(current, halves, half).reshape(-1, width), norm_attn)
    query = jnp.dot(normed, w_query, preferred_element_type=jnp.float32).astype(jnp.bfloat16)
    fresh = jnp.dot(normed, w_keyval, preferred_element_type=jnp.float32).astype(jnp.bfloat16)
    answers = attend(table - device * pool.shape[0], length, pool, query, fresh, marks)
    answers = answers.reshape(BEAMS, steps * rows, heads * head_dim)
    attended = shared_sum(place_block(answers, halves, half), 2).reshape(-1, heads * head_dim)
    residual = (
        current.reshape(-1, width).astype(jnp.float32)
        + jnp.dot(attended, w_out, preferred_element_type=jnp.float32)
    ).astype(jnp.bfloat16)
    terms = feed_forward(rms_round(residual, norm_mlp), w_gate, w_up, w_down)
    terms = terms.astype(jnp.bfloat16).reshape(kv_count, steps * rows, width)
    summed = reduced(terms, 3)
    residual = lax.dynamic_slice_in_dim(residual, member * steps * rows, steps * rows, 0)
    finished = (residual.astype(jnp.float32) + summed).astype(jnp.bfloat16)
    finished = finished.reshape(steps, rows, width)
    return reordered(by_target, swap(reordered(by_anchor.T, finished)))


def solution(mesh):
    in_specs = (
        P(None, ("req", "kv"), None),
        P(),
        P(),
        P(),
        P(("req", "kv"), None),
        P(("req", "kv"), None, None),
        P(),
        P(),
        P(),
        P(),
        P(),
        P(None, "kv"),
        P(None, "kv"),
        P("kv", None),
    )
    out_specs = P(None, ("req", "kv"), None)
    return jax.shard_map(
        on_device, mesh=mesh, in_specs=in_specs, out_specs=out_specs, check_vma=False
    )
```
